256 devices in a mesh: len: 16 (over y, x), chan: 16 (over z, core).
Axes of the slice: x: 4, y: 4, z: 8, core: 2. Of those that a mesh axis runs over, the one named last changes fastest.
Arguments:
- inputs: bfloat16 [2048, 32768], P(None, ('len', 'chan')), may hold values from -6 to 6
- grad_output: bfloat16 [2048, 32768], P(None, ('len', 'chan')), may hold values from -6 to 6
- pole_values: float32 [2048, 16], P('chan'), may hold values from 0.94 to 0.99998474, as said below
- residue_values: float32 [2048, 16], P('chan'), may hold values from -0.25 to 0.25
Outputs:
- input_grad: bfloat16 [2048, 32768], P(None, ('len', 'chan'))
- residue_grad: float32 [2048, 16], P('chan')
- pole_grad: float32 [2048, 16], P('chan')
The draws below stay inside these ranges and needn't reach their ends.
Inputs may be any that keep to these rules, and one draw needn't show every extreme that they name: `pole_values`: 1 - pole lies between 1 / 65536 and 0.06.
All inputs are finite; a program needn't handle non-finite values.
Results may differ from the reference program's by a relative error of at most 0.00105.
Values may be sent and summed in bfloat16 or wider, within the bound.
No kernel may reach another device: no remote copies, remote signals or barrier semaphores. Data moves between devices by JAX's collectives and lax.ppermute only.
A program may use at most 256 MiB of HBM per device.

```python
import math
import jax
import jax.numpy as jnp
from jax import lax

CH = 2048
P_SIZE = 16
BLOCK = 128
TOKENS = 32768


def log_between(base_key, array_shape, lower_end, upper_end):
    spread = jax.random.uniform(base_key, array_shape, jnp.float32)
    return jnp.exp(math.log(lower_end) + spread * (math.log(upper_end) - math.log(lower_end)))


def permute_rows(table, slot_order):
    return jnp.take_along_axis(table, slot_order, axis=1)


def mode_layout(base_key, single_low, single_high, middle_low, middle_high, quick_low, quick_high, pair_low, pair_high):
    key_list = jax.random.split(jax.random.fold_in(base_key, 101), 7)
    single_count = P_SIZE // 8
    quick_count = P_SIZE // 8
    pair_count = (P_SIZE - single_count) // 2
    middle_count = pair_count - quick_count
    single_rate = log_between(key_list[0], (CH, single_count), single_low, single_high)
    middle_base = log_between(key_list[1], (CH, middle_count), middle_low, middle_high)
    quick_base = log_between(key_list[2], (CH, quick_count), quick_low, quick_high)
    base_rate = jnp.concatenate([middle_base, quick_base], axis=1)
    rate_ratio = jax.random.uniform(key_list[3], (CH, pair_count), jnp.float32, 1.06, 1.14)
    magnitude = jax.random.uniform(key_list[4], (CH, pair_count), jnp.float32, pair_low, pair_high)
    sign_values = (2 * jax.random.randint(key_list[5], (CH, pair_count), 0, 2) - 1).astype(jnp.float32)
    pair_residue = magnitude * sign_values
    mode_rates = jnp.concatenate([single_rate, base_rate, base_rate * rate_ratio], axis=1)
    residues = jnp.concatenate([jnp.zeros((CH, single_count), jnp.float32), pair_residue, -pair_residue], axis=1)
    single_flag = jnp.concatenate([jnp.ones((CH, single_count), jnp.float32), jnp.zeros((CH, 2 * pair_count), jnp.float32)], axis=1)
    slot_order = jax.vmap(lambda one_key: jax.random.permutation(one_key, P_SIZE))(jax.random.split(key_list[6], CH))
    return (permute_rows(mode_rates, slot_order), permute_rows(residues, slot_order), permute_rows(single_flag, slot_order))


def draw_pole_values(key, part):
    mode_rates, residues, single_flag = mode_layout(key, 0.5 / TOKENS, 4.0 / TOKENS, 0.0036, 0.004, 0.02, 0.052, 0.12, 0.25)
    return 1.0 - mode_rates


def draw_residue_values(key, part):
    own_key = jax.random.fold_in(key, 5)
    mode_rates, residues, single_flag = mode_layout(key, 0.5 / TOKENS, 4.0 / TOKENS, 0.0036, 0.004, 0.02, 0.052, 0.12, 0.25)
    noise_draw = 0.08 * jax.random.truncated_normal(own_key, -3.0, 3.0, (CH, P_SIZE), jnp.float32)
    mode_width = mode_rates * (2.0 - mode_rates)
    return residues + single_flag * noise_draw * jnp.sqrt(mode_width)


def block_scale(stream_key, shape, cuts, least, largest):
    def one(axis_at, parts):
        heights = jax.random.uniform(jax.random.fold_in(jax.random.fold_in(stream_key, 6), axis_at), (parts,), jnp.float32, least / len(cuts), largest / len(cuts))
        return jnp.repeat(jnp.exp(heights), shape[axis_at] // parts).reshape((-1,) + (1,) * (len(shape) - axis_at - 1))

    level = one(*cuts[0])
    for cut in cuts[1:]:
        level = level * one(*cut)
    return level


def normal_values(rng, dims, deviation, most, shards=(), kind=jnp.bfloat16):
    entries = deviation * jax.random.normal(rng, dims, jnp.float32)
    if shards:
        entries = entries * block_scale(rng, dims, shards, -0.22, 0.18)
    return jnp.clip(entries, -most, most).astype(kind)


def setup_inputs(seed: int = 0) -> dict:
    seeds = jax.random.split(jax.random.key(seed), 5)
    return {
        "inputs": normal_values(seeds[0], (CH, TOKENS), 1.0, 6.0, ((1, 256),)),
        "grad_output": normal_values(seeds[1], (CH, TOKENS), 1.0, 6.0, ((1, 256),)),
        "pole_values": draw_pole_values(jax.random.fold_in(seeds[4], 71), 0),
        "residue_values": draw_residue_values(jax.random.fold_in(seeds[4], 71), 0),
    }


PRECISE = lax.Precision.HIGHEST

def link_pairs(earlier, latter):
    return (earlier[0] * latter[0], latter[0] * earlier[1] + latter[1])

def log_rates(pole_values):
    return jnp.log1p(-(1.0 - pole_values))

def finish_span(intra_state, intra_adjoint, output_blocks, pole_values, residue_values, state_in, adjoint_after):
    block_len = intra_state.shape[3]
    log_rate = log_rates(pole_values)[:, :, None]
    offsets = jnp.arange(block_len, dtype=jnp.float32)
    whole_step = jnp.broadcast_to(jnp.exp(log_rate * block_len), intra_state.shape[:3])
    forward_seq = jnp.concatenate([state_in[:, :, None], intra_state[:, :, :-1, -1]], axis=2)
    state_start = lax.associative_scan(link_pairs, (whole_step, forward_seq), axis=2)[1]
    backward_seq = jnp.concatenate([intra_adjoint[:, :, 1:, 0], adjoint_after[:, :, None]], axis=2)
    adjoint_next = lax.associative_scan(link_pairs, (whole_step, backward_seq), reverse=True, axis=2)[1]
    rate_four = log_rate[..., None]
    state_full = intra_state + jnp.exp(rate_four * (offsets + 1.0)) * state_start[..., None]
    shifted = jnp.concatenate([jnp.zeros_like(intra_state[..., :1]), intra_state[..., :-1]], axis=3)
    previous = shifted + jnp.exp(rate_four * offsets) * state_start[..., None]
    adjoint = intra_adjoint + jnp.exp(rate_four * (block_len - offsets)) * adjoint_next[..., None]
    residue_raw = jnp.einsum('cpnt,cnt->cp', state_full, output_blocks, precision=PRECISE)
    pole_raw = residue_values * lax.optimization_barrier(jnp.sum(adjoint * previous, axis=(2, 3)))
    input_grad = jnp.einsum('cp,cpnt->cnt', residue_values, adjoint, precision=PRECISE)
    return (input_grad, residue_raw, pole_raw)

def span_pass(input_blocks, output_blocks, pole_values, residue_values, state_in, adjoint_after):
    block_len = input_blocks.shape[2]
    log_rate = log_rates(pole_values)[:, :, None, None]
    offsets = jnp.arange(block_len, dtype=jnp.float32)
    decay_up = jnp.exp(log_rate * offsets)
    growth = jnp.exp(-log_rate * offsets)
    intra_state = decay_up * jnp.cumsum(input_blocks[:, None] * growth, axis=3)
    flipped = jnp.flip(output_blocks[:, None] * decay_up, axis=3)
    intra_adjoint = growth * jnp.flip(jnp.cumsum(flipped, axis=3), axis=3)
    return finish_span(intra_state, intra_adjoint, output_blocks, pole_values, residue_values, state_in, adjoint_after)

def scale_grads(residue_raw, pole_raw, pole_values, token_total):
    mode_width = (1.0 - pole_values) * (1.0 + pole_values)
    root_total = math.sqrt(token_total)
    return (residue_raw * jnp.sqrt(mode_width) / root_total, pole_raw * mode_width / root_total)

def reference(inputs, grad_output, pole_values, residue_values):
    group_size = math.gcd(CH, 16)
    groups = CH // group_size
    block_count = TOKENS // BLOCK
    input_rows = inputs.astype(jnp.float32).reshape(groups, group_size, block_count, BLOCK)
    output_rows = grad_output.astype(jnp.float32).reshape(groups, group_size, block_count, BLOCK)
    pole_groups = pole_values.reshape(groups, group_size, P_SIZE)
    residue_groups = residue_values.reshape(groups, group_size, P_SIZE)

    def one_group(packed):
        input_blocks, output_blocks, poles_here, residues_here = packed
        zero_state = jnp.zeros(poles_here.shape, jnp.float32)
        return span_pass(input_blocks, output_blocks, poles_here, residues_here, zero_state, zero_state)
    input_grad, residue_raw, pole_raw = lax.map(one_group, (input_rows, output_rows, pole_groups, residue_groups))
    input_grad = input_grad.reshape(CH, TOKENS).astype(jnp.bfloat16)
    residue_grad, pole_grad = scale_grads(residue_raw.reshape(CH, P_SIZE), pole_raw.reshape(CH, P_SIZE), pole_values, TOKENS)
    return (input_grad, residue_grad, pole_grad)
```

```python
import functools
import math

import jax
import jax.numpy as jnp
from jax import lax
from jax.experimental import pallas as pl
from jax.experimental.pallas import tpu as pltpu
from jax.sharding import PartitionSpec as P

ROWS = 8
GROUP = 8
F32 = jnp.float32
VMEM = pl.BlockSpec(memory_space=pltpu.VMEM)


def identity_matrix(size):
    rows = lax.broadcasted_iota(jnp.int32, (size, size), 0)
    cols = lax.broadcasted_iota(jnp.int32, (size, size), 1)
    return (rows == cols).astype(F32).astype(jnp.bfloat16)


def flip(eye, tile):
    return lax.dot_general(eye, tile, (((1,), (1,)), ((), ())), preferred_element_type=F32)


def flip_blocks(src_ref, dst_ref):
    blocks, chans, block_len = src_ref.shape
    eye = identity_matrix(block_len)
    for n in range(blocks):
        dst_ref[pl.ds(n, block_len, stride=blocks), :] = flip(eye, src_ref[n])


def log_rates(poles):
    return jnp.log1p(-(1.0 - poles))


def spread(table, p):
    return jnp.broadcast_to(table[p : p + 1, :], (ROWS, table.shape[1]))


def cleared(ref, count):
    ref[:ROWS, :] = jnp.zeros((ROWS, ref.shape[1]), F32)
    return (ref[:ROWS, :],) * count


def block_rows(ref, n, blocks, modes):
    return ref[pl.ds(n, modes, stride=blocks), :]


def ends_kernel(blocks, spans, g_ref, pole_ref, res_ref, gt_ref, coef_ref, h_ref, hs_ref, pad_ref):
    modes = pole_ref.shape[1]
    chans = pole_ref.shape[0]
    block_len = g_ref.shape[2]
    pad_ref[:, :modes] = pole_ref[...]
    pad_ref[:, modes : 2 * modes] = res_ref[...]
    coef_ref[...] = pad_ref[...].T[: 2 * modes, :]
    lam = coef_ref[:modes, :]
    flip_blocks(g_ref, gt_ref)
    empty = cleared(h_ref, modes)
    for half in range(blocks // ROWS):
        wide = [spread(lam, p) for p in range(modes)]

        def step(i, held):
            at = pl.multiple_of((block_len - 1 - i) * blocks + half * ROWS, ROWS)
            g = gt_ref[pl.ds(at, ROWS), :]
            return tuple(l * a + g for l, a in zip(wide, held))

        ends = lax.fori_loop(0, block_len, step, empty, unroll=8)
        for p in range(modes):
            h_ref[p * blocks + half * ROWS : p * blocks + half * ROWS + ROWS, :] = ends[p]
    block_step = jnp.exp(block_len * log_rates(lam))
    total = block_rows(h_ref, blocks - 1, blocks, modes)
    for n in range(blocks - 2, -1, -1):
        total = block_step * total + block_rows(h_ref, n, blocks, modes)
    for span in range(spans):
        hs_ref[span] = total


def input_grad_kernel(blocks, spans, gt_ref, coef_ref, h_ref, got_ref, out_ref, next_ref, flat_ref):
    modes = coef_ref.shape[0] // 2
    chans = coef_ref.shape[1]
    block_len = gt_ref.shape[0] // blocks
    lam = coef_ref[:modes, :]
    res = coef_ref[modes:, :]
    rate = log_rates(lam)
    block_step = jnp.exp(block_len * rate)
    span_step = jnp.exp((blocks * block_len) * rate)
    place = lax.axis_index("len")
    total = jnp.zeros((modes, chans), F32)
    for span in range(spans - 1, 0, -1):
        total = jnp.where(span > place, span_step * total + got_ref[span], total)
    for n in range(blocks - 1, -1, -1):
        next_ref[pl.ds(n, modes, stride=blocks), :] = total
        total = block_step * total + block_rows(h_ref, n, blocks, modes)
    for half in range(blocks // ROWS):
        wide = [spread(lam, p) for p in range(modes)]
        gain = [spread(res, p) for p in range(modes)]
        start = tuple(
            next_ref[p * blocks + half * ROWS : p * blocks + half * ROWS + ROWS, :]
            for p in range(modes)
        )

        def step(i, held):
            at = pl.multiple_of((block_len - 1 - i) * blocks + half * ROWS, ROWS)
            g = gt_ref[pl.ds(at, ROWS), :]
            held = tuple(l * a + g for l, a in zip(wide, held))
            terms = [r * a for r, a in zip(gain, held)]
            while len(terms) > 1:
                terms = [a + b for a, b in zip(terms[::2], terms[1::2])]
            flat_ref[pl.ds(at, ROWS), :] = terms[0]
            return held

        lax.fori_loop(0, block_len, step, start, unroll=4)
    eye = identity_matrix(chans)
    for n in range(blocks):
        tile = flat_ref[pl.ds(n, block_len, stride=blocks), :].astype(jnp.bfloat16)
        out_ref[n] = flip(eye, tile).astype(jnp.bfloat16)


def sums_kernel(
    blocks, spans, x_ref, gt_ref, coef_ref, h_ref, pay_ref, xt_ref, s_ref, d_ref, r_ref, q_ref, t_ref, zero_ref
):
    modes = coef_ref.shape[0] // 2
    chans = coef_ref.shape[1]
    block_len = gt_ref.shape[0] // blocks
    lam = coef_ref[:modes, :]
    flip_blocks(x_ref, xt_ref)
    empty = cleared(zero_ref, GROUP)
    for half in range(blocks // ROWS):
        for first in range(0, modes, GROUP):
            wide = [spread(lam, first + k) for k in range(GROUP)]

            def ahead(i, held):
                at = pl.multiple_of(i * blocks + half * ROWS, ROWS)
                g = gt_ref[pl.ds(at, ROWS), :]
                x = xt_ref[pl.ds(at, ROWS), :]
                state, slope, res_sum, pole_sum = held
                slope = tuple(l * d + s for l, d, s in zip(wide, slope, state))
                state = tuple(l * s + x for l, s in zip(wide, state))
                res_sum = tuple(r + g * s for r, s in zip(res_sum, state))
                pole_sum = tuple(q + g * d for q, d in zip(pole_sum, slope))
                return (state, slope, res_sum, pole_sum)

            results = lax.fori_loop(0, block_len, ahead, (empty,) * 4, unroll=4)

            def back(i, held):
                at = pl.multiple_of((block_len - 1 - i) * blocks + half * ROWS, ROWS)
                g = gt_ref[pl.ds(at, ROWS), :]
                adjoint, weighted = held
                adjoint = tuple(l * a + g for l, a in zip(wide, adjoint))
                weighted = tuple(l * q + a for l, q, a in zip(wide, weighted, adjoint))
                return (adjoint, weighted)

            weighted = lax.fori_loop(0, block_len, back, (empty,) * 2, unroll=4)[1]
            for k in range(GROUP):
                rows = slice(
                    (first + k) * blocks + half * ROWS, (first + k) * blocks + half * ROWS + ROWS
                )
                s_ref[rows, :] = results[0][k]
                d_ref[rows, :] = results[1][k]
                r_ref[rows, :] = results[2][k]
                q_ref[rows, :] = results[3][k]
                t_ref[rows, :] = weighted[k]
    rate = log_rates(lam)
    block_step = jnp.exp(block_len * rate)
    block_slope = block_len * jnp.exp((block_len - 1) * rate)
    rows_of = lambda ref, n: block_rows(ref, n, blocks, modes)
    state = jnp.zeros((modes, chans), F32)
    slope = state
    res_sum = state
    pole_sum = state
    for n in range(blocks):
        after = lam * rows_of(h_ref, n)
        res_sum = res_sum + (rows_of(r_ref, n) + state * after)
        pole_sum = pole_sum + (rows_of(q_ref, n) + slope * after + state * rows_of(t_ref, n))
        slope = block_step * slope + block_slope * state + rows_of(d_ref, n)
        state = block_step * state + rows_of(s_ref, n)
    total = jnp.zeros((modes, chans), F32)
    weighted = total
    for n in range(blocks - 1, -1, -1):
        weighted = block_step * (weighted + block_len * total) + rows_of(t_ref, n)
        total = block_step * total + rows_of(h_ref, n)
    for span in range(spans):
        for k, item in enumerate((state, slope, res_sum, pole_sum, weighted)):
            pay_ref[span, k * modes : (k + 1) * modes, :] = item


def finish_kernel(spans, span_len, pay_ref, got_ref, coef_ref, res_out, pole_out, pad_ref):
    modes = coef_ref.shape[0] // 2
    lam = coef_ref[:modes, :]
    res = coef_ref[modes:, :]
    rate = log_rates(lam)
    span_step = jnp.exp(span_len * rate)
    span_slope = span_len * jnp.exp((span_len - 1) * rate)
    state = jnp.zeros(lam.shape, F32)
    slope = state
    res_sum = state
    pole_sum = state
    for span in range(spans):
        ends, slopes, res_part, pole_part, weighted = [
            pay_ref[span, k * modes : (k + 1) * modes, :] for k in range(5)
        ]
        after = lam * got_ref[span]
        res_sum = res_sum + (res_part + state * after)
        pole_sum = pole_sum + (pole_part + slope * after + state * weighted)
        slope = span_step * slope + span_slope * state + slopes
        state = span_step * state + ends
    width = (1.0 - lam) * (1.0 + lam)
    scale = 1.0 / math.sqrt(spans * span_len)
    pad_ref[:modes, :] = res_sum * jnp.sqrt(width) * scale
    pad_ref[modes : 2 * modes, :] = res * pole_sum * width * scale
    turned = pad_ref[...].T
    res_out[...] = turned[:, :modes]
    pole_out[...] = turned[:, modes : 2 * modes]


def call(kernel, out_shape, in_count, scratch, name, flops):
    single = not isinstance(out_shape, (tuple, list))
    return pl.pallas_call(
        kernel,
        out_shape=out_shape,
        in_specs=[VMEM] * in_count,
        out_specs=VMEM if single else [VMEM] * len(out_shape),
        scratch_shapes=scratch,
        compiler_params=pltpu.CompilerParams(vmem_limit_bytes=32 * 1024 * 1024),
        cost_estimate=pl.CostEstimate(flops=flops, bytes_accessed=2**20, transcendentals=0),
        name=name,
    )


def swap(part, axis):
    return lax.all_to_all(part, axis, split_axis=0, concat_axis=0, tiled=True)


def body(inputs, grad_output, pole_values, residue_values):
    spans = lax.axis_size("len")
    blocks = lax.axis_size("chan")
    chans, modes = pole_values.shape
    block_len = inputs.shape[1]
    flat = blocks * block_len
    held = modes * blocks
    work = chans * flat * modes
    shape = lambda *dims: jax.ShapeDtypeStruct(dims, F32)
    scratch = lambda *dims: pltpu.VMEM(dims, F32)
    moved_grads = swap(grad_output.reshape(blocks, chans, block_len), "chan")
    moved_inputs = swap(inputs.reshape(blocks, chans, block_len), "chan")
    flat_grads, coef, ends, span_ends = call(
        functools.partial(ends_kernel, blocks, spans),
        (shape(flat, chans), shape(2 * modes, chans), shape(held, chans), shape(spans, modes, chans)),
        3,
        [scratch(chans, chans)],
        "block_ends",
        2 * work,
    )(moved_grads, pole_values, residue_values)
    all_ends = swap(span_ends, "len")
    rounded = call(
        functools.partial(input_grad_kernel, blocks, spans),
        jax.ShapeDtypeStruct((blocks, chans, block_len), jnp.bfloat16),
        4,
        [scratch(held, chans), scratch(flat, chans)],
        "input_grad",
        4 * work,
    )(flat_grads, coef, ends, all_ends)
    input_grad = swap(rounded, "chan").reshape(blocks * chans, block_len)
    pay = call(
        functools.partial(sums_kernel, blocks, spans),
        shape(spans, 5 * modes, chans),
        4,
        [scratch(flat, chans)] + [scratch(held, chans)] * 5 + [scratch(ROWS, chans)],
        "mode_sums",
        12 * work,
    )(moved_inputs, flat_grads, coef, ends)
    all_pay = swap(pay, "len")
    residue_grad, pole_grad = call(
        functools.partial(finish_kernel, spans, flat),
        (shape(chans, modes), shape(chans, modes)),
        3,
        [scratch(chans, chans)],
        "finish",
        work // 100,
    )(all_pay, all_ends, coef)
    return (input_grad, residue_grad, pole_grad)


def solution(mesh):
    in_specs = (
        P(None, ("len", "chan")),
        P(None, ("len", "chan")),
        P("chan", None),
        P("chan", None),
    )
    out_specs = (P(None, ("len", "chan")), P("chan", None), P("chan", None))
    return jax.shard_map(body, mesh=mesh, in_specs=in_specs, out_specs=out_specs, check_vma=False)
```

```python
import functools
import math

import jax
import jax.numpy as jnp
from jax import lax
from jax.experimental import pallas as pl
from jax.experimental.pallas import tpu as pltpu
from jax.sharding import PartitionSpec as P

ROWS = 8
GROUP = 8
F32 = jnp.float32
VMEM = pl.BlockSpec(memory_space=pltpu.VMEM)


def identity_matrix(size):
    rows = lax.broadcasted_iota(jnp.int32, (size, size), 0)
    cols = lax.broadcasted_iota(jnp.int32, (size, size), 1)
    return (rows == cols).astype(F32).astype(jnp.bfloat16)


def flip(eye, tile):
    return lax.dot_general(eye, tile, (((1,), (1,)), ((), ())), preferred_element_type=F32)


def flip_blocks(src_ref, dst_ref):
    blocks, _, block_len = src_ref.shape
    eye = identity_matrix(block_len)
    for n in range(blocks):
        dst_ref[pl.ds(n, block_len, stride=blocks), :] = flip(eye, src_ref[n])


def log_rates(poles):
    return jnp.log1p(-(1.0 - poles))


def spread(ref, p):
    return jnp.broadcast_to(ref[p : p + 1, :], (ROWS, ref.shape[1]))


def cleared(ref, count):
    ref[:ROWS, :] = jnp.zeros((ROWS, ref.shape[1]), F32)
    return (ref[:ROWS, :],) * count


def block_rows(ref, n, blocks, modes):
    return ref[pl.ds(n, modes, stride=blocks), :]


def ends_kernel(blocks, moved_ref, lam_ref, gt_ref, h_ref, head_ref):
    modes = lam_ref.shape[0]
    block_len = moved_ref.shape[2]
    flip_blocks(moved_ref, gt_ref)
    empty = cleared(h_ref, modes)
    for half in range(blocks // ROWS):
        wide = [spread(lam_ref, p) for p in range(modes)]

        def back(i, held):
            at = pl.multiple_of((block_len - 1 - i) * blocks + half * ROWS, ROWS)
            g = gt_ref[pl.ds(at, ROWS), :]
            return tuple(l * a + g for l, a in zip(wide, held))

        ends = lax.fori_loop(0, block_len, back, empty, unroll=8)
        for p in range(modes):
            at = p * blocks + half * ROWS
            h_ref[at : at + ROWS, :] = ends[p]
    step = jnp.exp(block_len * log_rates(lam_ref[...]))
    head_ref[...] = folded(step, [block_rows(h_ref, n, blocks, modes) for n in range(blocks)])


def folded(step, heads):
    total = heads[-1]
    for head in heads[-2::-1]:
        total = step * total + head
    return total


def weighted_kernel(blocks, gt_ref, lam_ref, t_ref):
    modes = lam_ref.shape[0]
    block_len = gt_ref.shape[0] // blocks
    empty = cleared(t_ref, GROUP)
    for half in range(blocks // ROWS):
        for first in range(0, modes, GROUP):
            wide = [spread(lam_ref, first + k) for k in range(GROUP)]

            def back(i, held):
                at = pl.multiple_of((block_len - 1 - i) * blocks + half * ROWS, ROWS)
                g = gt_ref[pl.ds(at, ROWS), :]
                adjoint, weighted = held
                adjoint = tuple(l * a + g for l, a in zip(wide, adjoint))
                weighted = tuple(l * q + a for l, q, a in zip(wide, weighted, adjoint))
                return (adjoint, weighted)

            weighted = lax.fori_loop(0, block_len, back, (empty,) * 2, unroll=8)[1]
            for k in range(GROUP):
                at = (first + k) * blocks + half * ROWS
                t_ref[at : at + ROWS, :] = weighted[k]


def near_kernel(span_len, *refs):
    *parts, lam_ref, _, all_ref, near_ref, group_ref = refs
    count = len(parts)
    place = lax.rem(lax.axis_index("len"), count)
    heads = ordered(parts, place, all_ref)
    step = jnp.exp(span_len * log_rates(lam_ref[...]))
    group_ref[...] = folded(step, heads)
    near_ref[...] = folded_after(step, heads, place)


def folded_after(step, heads, place):
    total = jnp.zeros(step.shape, F32)
    for i in range(len(heads) - 1, 0, -1):
        total = jnp.where(i > place, step * total + heads[i], total)
    return total


def input_grad_kernel(blocks, inner, outer, *refs):
    *parts, near_ref, gt_ref, lam_ref, res_ref, h_ref, _, out_ref, all_ref, next_ref, flat_ref = refs
    modes, chans = lam_ref.shape
    block_len = gt_ref.shape[0] // blocks
    span_len = blocks * block_len
    rate = log_rates(lam_ref[...])
    block_step = jnp.exp(block_len * rate)
    place = lax.axis_index("len")
    at_inner = lax.rem(place, inner)
    at_outer = lax.div(place, inner)
    heads = ordered(parts, at_outer, all_ref)
    far = folded_after(jnp.exp((inner * span_len) * rate), heads, at_outer)
    reach = (span_len * (inner - 1 - at_inner)).astype(F32)
    total = near_ref[...] + jnp.exp(reach * rate) * far
    for n in range(blocks - 1, -1, -1):
        next_ref[pl.ds(n, modes, stride=blocks), :] = total
        total = block_step * total + block_rows(h_ref, n, blocks, modes)
    for half in range(blocks // ROWS):
        wide = [spread(lam_ref, p) for p in range(modes)]
        gain = [spread(res_ref, p) for p in range(modes)]
        start = tuple(
            next_ref[p * blocks + half * ROWS : p * blocks + half * ROWS + ROWS, :]
            for p in range(modes)
        )

        def step(i, held):
            at = pl.multiple_of((block_len - 1 - i) * blocks + half * ROWS, ROWS)
            g = gt_ref[pl.ds(at, ROWS), :]
            held = tuple(l * a + g for l, a in zip(wide, held))
            terms = [r * a for r, a in zip(gain, held)]
            while len(terms) > 1:
                terms = [a + b for a, b in zip(terms[::2], terms[1::2])]
            flat_ref[pl.ds(at, ROWS), :] = terms[0]
            return held

        lax.fori_loop(0, block_len, step, start, unroll=4)
    eye = identity_matrix(chans)
    for n in range(blocks):
        tile = flat_ref[pl.ds(n, block_len, stride=blocks), :].astype(jnp.bfloat16)
        out_ref[n] = flip(eye, tile).astype(jnp.bfloat16)


def mode_sums(first, blocks, x_ref, gt_ref, lam_ref, h_ref, t_ref, parts_refs):
    block_len = gt_ref.shape[0] // blocks
    lam = lam_ref[first : first + GROUP, :]
    empty = cleared(parts_refs[0], GROUP)
    wide = [spread(lam_ref, first + k) for k in range(GROUP)]
    for half in range(blocks // ROWS):

        def ahead(i, held):
            at = pl.multiple_of(i * blocks + half * ROWS, ROWS)
            g = gt_ref[pl.ds(at, ROWS), :]
            x = x_ref[pl.ds(at, ROWS), :]
            state, slope, res_sum, pole_sum = held
            slope = tuple(l * d + s for l, d, s in zip(wide, slope, state))
            state = tuple(l * s + x for l, s in zip(wide, state))
            res_sum = tuple(r + g * s for r, s in zip(res_sum, state))
            pole_sum = tuple(q + g * d for q, d in zip(pole_sum, slope))
            return (state, slope, res_sum, pole_sum)

        results = lax.fori_loop(0, block_len, ahead, (empty,) * 4, unroll=8)
        for k in range(GROUP):
            at = k * blocks + half * ROWS
            for ref, result in zip(parts_refs, results):
                ref[at : at + ROWS, :] = result[k]
    rate = log_rates(lam)
    block_step = jnp.exp(block_len * rate)
    block_slope = block_len * jnp.exp((block_len - 1) * rate)
    own = lambda ref, n: ref[pl.ds(n, GROUP, stride=blocks), :]
    of_all = lambda ref, n: ref[pl.ds(first * blocks + n, GROUP, stride=blocks), :]
    s_ref, d_ref, r_ref, q_ref = parts_refs
    state, slope, res_sum, pole_sum, total, weighted = [jnp.zeros(lam.shape, F32)] * 6
    for n in range(blocks):
        after = lam * of_all(h_ref, n)
        res_sum = res_sum + (own(r_ref, n) + state * after)
        pole_sum = pole_sum + (own(q_ref, n) + slope * after + state * of_all(t_ref, n))
        slope = block_step * slope + block_slope * state + own(d_ref, n)
        state = block_step * state + own(s_ref, n)
    for n in range(blocks - 1, -1, -1):
        weighted = block_step * (weighted + block_len * total) + of_all(t_ref, n)
        total = block_step * total + of_all(h_ref, n)
    return state, slope, res_sum, pole_sum, weighted


def sums_first_kernel(blocks, moved_ref, gt_ref, lam_ref, h_ref, t_ref, xt_ref, pay_ref, *parts):
    flip_blocks(moved_ref, xt_ref)
    for k, item in enumerate(mode_sums(0, blocks, xt_ref, gt_ref, lam_ref, h_ref, t_ref, parts)):
        pay_ref[k * GROUP : (k + 1) * GROUP, :] = item


def sums_rest_kernel(blocks, xt_ref, gt_ref, lam_ref, h_ref, t_ref, first_ref, _, pay_ref, *parts):
    modes = lam_ref.shape[0]
    for k in range(5):
        pay_ref[k * modes : k * modes + GROUP, :] = first_ref[k * GROUP : (k + 1) * GROUP, :]
    for first in range(GROUP, modes, GROUP):
        items = mode_sums(first, blocks, xt_ref, gt_ref, lam_ref, h_ref, t_ref, parts)
        for k, item in enumerate(items):
            pay_ref[k * modes + first : k * modes + first + GROUP, :] = item


def ordered(refs, place, slots_ref):
    count = len(refs)
    for s, ref in enumerate(refs):
        slots_ref[lax.rem(place + count - s, count)] = ref[...]
    return [slots_ref[i] for i in range(count)]


def joined(lam, length, parts, heads):
    modes = lam.shape[0]
    rate = log_rates(lam)
    step = jnp.exp(length * rate)
    slope_step = length * jnp.exp((length - 1) * rate)
    state, slope, res_sum, pole_sum = [jnp.zeros(lam.shape, F32)] * 4
    tables = [[part[k * modes : (k + 1) * modes, :] for k in range(5)] for part in parts]
    for (ends, slopes, res_part, pole_part, weighted), head in zip(tables, heads):
        after = lam * head
        res_sum = res_sum + (res_part + state * after)
        pole_sum = pole_sum + (pole_part + slope * after + state * weighted)
        slope = step * slope + slope_step * state + slopes
        state = step * state + ends
    total = jnp.zeros(lam.shape, F32)
    weighted = total
    for table, head in zip(tables[::-1], heads[::-1]):
        weighted = step * (weighted + length * total) + table[4]
        total = step * total + head
    return state, slope, res_sum, pole_sum, weighted


def join_kernel(span_len, *refs):
    *parts, heads_ref, lam_ref, pay_ref, slots_ref = refs
    modes = lam_ref.shape[0]
    count = len(parts)
    parts = ordered(parts, lax.rem(lax.axis_index("len"), count), slots_ref)
    heads = [heads_ref[i] for i in range(count)]
    for k, item in enumerate(joined(lam_ref[...], span_len, parts, heads)):
        pay_ref[k * modes : (k + 1) * modes, :] = item


def finish_kernel(inner, group_len, *refs):
    *parts, heads_ref, lam_ref, res_ref, res_out, pole_out, slots_ref = refs
    count = len(parts)
    lam = lam_ref[...]
    parts = ordered(parts, lax.div(lax.axis_index("len"), inner), slots_ref)
    heads = [heads_ref[i] for i in range(count)]
    _, _, res_sum, pole_sum, _ = joined(lam, group_len, parts, heads)
    width = (1.0 - lam) * (1.0 + lam)
    scale = 1.0 / math.sqrt(count * group_len)
    res_out[...] = res_sum * jnp.sqrt(width) * scale
    pole_out[...] = res_ref[...] * pole_sum * width * scale


def call(kernel, out_shape, in_count, scratch, name, flops):
    single = not isinstance(out_shape, (tuple, list))
    return pl.pallas_call(
        kernel,
        out_shape=out_shape,
        in_specs=[VMEM] * in_count,
        out_specs=VMEM if single else [VMEM] * len(out_shape),
        scratch_shapes=scratch,
        compiler_params=pltpu.CompilerParams(vmem_limit_bytes=32 * 1024 * 1024),
        cost_estimate=pl.CostEstimate(flops=flops, bytes_accessed=2**20, transcendentals=0),
        name=name,
    )


def swap(part, axis):
    return lax.all_to_all(part, axis, split_axis=0, concat_axis=0, tiled=True)


def rotated(part, count, stride, spans):
    size = count * stride
    hop = lambda i, s: (i // size) * size + (i % size + s * stride) % size
    return [
        lax.ppermute(part, "len", [(i, hop(i, s)) for i in range(spans)]) for s in range(1, count)
    ]


def body(inputs, grad_output, pole_values, residue_values):
    spans = lax.axis_size("len")
    blocks = lax.axis_size("chan")
    inner = math.isqrt(spans)
    outer = spans // inner
    chans, modes = pole_values.shape
    block_len = inputs.shape[1]
    flat = blocks * block_len
    held = modes * blocks
    work = chans * flat * modes
    shape = lambda *dims: jax.ShapeDtypeStruct(dims, F32)
    scratch = lambda *dims: pltpu.VMEM(dims, F32)
    cut = lambda part: part.reshape(blocks, chans, block_len)
    table = shape(modes, chans)
    poles = pole_values.T
    residues = residue_values.T
    moved_grads = swap(cut(grad_output), "chan")
    moved_inputs = swap(cut(inputs), "chan")
    flat_grads, ends, head = call(
        functools.partial(ends_kernel, blocks),
        (shape(flat, chans), shape(held, chans), table),
        2,
        [],
        "block_ends",
        2 * work,
    )(moved_grads, poles)
    weighted = call(
        functools.partial(weighted_kernel, blocks),
        shape(held, chans),
        2,
        [],
        "weighted",
        4 * work,
    )(flat_grads, poles)
    heads, near, group_head = call(
        functools.partial(near_kernel, flat),
        (shape(inner, modes, chans), table, table),
        inner + 2,
        [],
        "near",
        work // 100,
    )(head, *rotated(head, inner, 1, spans), poles, weighted)
    flat_inputs, first_pay = call(
        functools.partial(sums_first_kernel, blocks),
        (shape(flat, chans), shape(5 * GROUP, chans)),
        5,
        [scratch(GROUP * blocks, chans)] * 4,
        "sums_first",
        4 * work,
    )(moved_inputs, flat_grads, poles, ends, weighted)
    rounded, group_heads = call(
        functools.partial(input_grad_kernel, blocks, inner, outer),
        (jax.ShapeDtypeStruct((blocks, chans, block_len), jnp.bfloat16), shape(outer, modes, chans)),
        outer + 6,
        [scratch(held, chans), scratch(flat, chans)],
        "input_grad",
        4 * work,
    )(
        group_head,
        *rotated(group_head, outer, inner, spans),
        near,
        flat_grads,
        poles,
        residues,
        ends,
        first_pay,
    )
    input_grad = swap(rounded, "chan").reshape(blocks * chans, block_len)
    pay = call(
        functools.partial(sums_rest_kernel, blocks),
        shape(5 * modes, chans),
        7,
        [scratch(GROUP * blocks, chans)] * 4,
        "sums_rest",
        4 * work,
    )(flat_inputs, flat_grads, poles, ends, weighted, first_pay, group_heads)
    group_pay = call(
        functools.partial(join_kernel, flat),
        shape(5 * modes, chans),
        inner + 2,
        [scratch(inner, 5 * modes, chans)],
        "join",
        work // 100,
    )(pay, *rotated(pay, inner, 1, spans), heads, poles)
    residue_grad, pole_grad = call(
        functools.partial(finish_kernel, inner, inner * flat),
        (table, table),
        outer + 3,
        [scratch(outer, 5 * modes, chans)],
        "finish",
        work // 100,
    )(group_pay, *rotated(group_pay, outer, inner, spans), group_heads, poles, residues)
    return (input_grad, residue_grad.T, pole_grad.T)


def solution(mesh):
    in_specs = (
        P(None, ("len", "chan")),
        P(None, ("len", "chan")),
        P("chan", None),
        P("chan", None),
    )
    out_specs = (P(None, ("len", "chan")), P("chan", None), P("chan", None))
    return jax.shard_map(body, mesh=mesh, in_specs=in_specs, out_specs=out_specs, check_vma=False)
```

```python
import functools
import math

import jax
import jax.numpy as jnp
from jax import lax
from jax.experimental import pallas as pl
from jax.experimental.pallas import tpu as pltpu
from jax.sharding import PartitionSpec as P

ROWS = 8
GROUP = 8
F32 = jnp.float32
VMEM = pl.BlockSpec(memory_space=pltpu.VMEM)


def identity_matrix(size):
    rows = lax.broadcasted_iota(jnp.int32, (size, size), 0)
    cols = lax.broadcasted_iota(jnp.int32, (size, size), 1)
    return (rows == cols).astype(F32).astype(jnp.bfloat16)


def flip(eye, tile):
    return lax.dot_general(eye, tile, (((1,), (1,)), ((), ())), preferred_element_type=F32)


def flip_blocks(src_ref, dst_ref):
    blocks, _, block_len = src_ref.shape
    eye = identity_matrix(block_len)
    for n in range(blocks):
        dst_ref[pl.ds(n, block_len, stride=blocks), :] = flip(eye, src_ref[n])


def log_rates(poles):
    return jnp.log1p(-(1.0 - poles))


def spread(ref, p):
    return jnp.broadcast_to(ref[p : p + 1, :], (ROWS, ref.shape[1]))


def cleared(ref, count):
    ref[:ROWS, :] = jnp.zeros((ROWS, ref.shape[1]), F32)
    return (ref[:ROWS, :],) * count


def block_rows(ref, n, blocks, modes):
    return ref[pl.ds(n, modes, stride=blocks), :]


def ends_kernel(blocks, spans, moved_ref, lam_ref, gt_ref, h_ref, head_ref):
    modes = lam_ref.shape[0]
    block_len = moved_ref.shape[2]
    flip_blocks(moved_ref, gt_ref)
    empty = cleared(h_ref, modes)
    for half in range(blocks // ROWS):
        wide = [spread(lam_ref, p) for p in range(modes)]

        def back(i, held):
            at = pl.multiple_of((block_len - 1 - i) * blocks + half * ROWS, ROWS)
            g = gt_ref[pl.ds(at, ROWS), :]
            return tuple(l * a + g for l, a in zip(wide, held))

        ends = lax.fori_loop(0, block_len, back, empty, unroll=8)
        for p in range(modes):
            at = p * blocks + half * ROWS
            h_ref[at : at + ROWS, :] = ends[p]
    step = jnp.exp(block_len * log_rates(lam_ref[...]))
    head = folded(step, [block_rows(h_ref, n, blocks, modes) for n in range(blocks)])
    for span in range(spans):
        head_ref[span] = head


def folded(step, heads):
    total = heads[-1]
    for head in heads[-2::-1]:
        total = step * total + head
    return total


def weighted_kernel(blocks, gt_ref, lam_ref, t_ref):
    modes = lam_ref.shape[0]
    block_len = gt_ref.shape[0] // blocks
    empty = cleared(t_ref, GROUP)
    for half in range(blocks // ROWS):
        for first in range(0, modes, GROUP):
            wide = [spread(lam_ref, first + k) for k in range(GROUP)]

            def back(i, held):
                at = pl.multiple_of((block_len - 1 - i) * blocks + half * ROWS, ROWS)
                g = gt_ref[pl.ds(at, ROWS), :]
                adjoint, weighted = held
                adjoint = tuple(l * a + g for l, a in zip(wide, adjoint))
                weighted = tuple(l * q + a for l, q, a in zip(wide, weighted, adjoint))
                return (adjoint, weighted)

            weighted = lax.fori_loop(0, block_len, back, (empty,) * 2, unroll=8)[1]
            for k in range(GROUP):
                at = (first + k) * blocks + half * ROWS
                t_ref[at : at + ROWS, :] = weighted[k]


def folded_after(step, heads, place):
    total = jnp.zeros(step.shape, F32)
    for i in range(len(heads) - 1, 0, -1):
        total = jnp.where(i > place, step * total + heads[i], total)
    return total


def input_grad_kernel(
    blocks, spans, heads_ref, gt_ref, lam_ref, res_ref, h_ref, _, out_ref, next_ref, flat_ref
):
    modes, chans = lam_ref.shape
    block_len = gt_ref.shape[0] // blocks
    rate = log_rates(lam_ref[...])
    block_step = jnp.exp(block_len * rate)
    span_step = jnp.exp((blocks * block_len) * rate)
    total = folded_after(span_step, [heads_ref[i] for i in range(spans)], lax.axis_index("len"))
    for n in range(blocks - 1, -1, -1):
        next_ref[pl.ds(n, modes, stride=blocks), :] = total
        total = block_step * total + block_rows(h_ref, n, blocks, modes)
    for half in range(blocks // ROWS):
        wide = [spread(lam_ref, p) for p in range(modes)]
        gain = [spread(res_ref, p) for p in range(modes)]
        start = tuple(
            next_ref[p * blocks + half * ROWS : p * blocks + half * ROWS + ROWS, :]
            for p in range(modes)
        )

        def step(i, held):
            at = pl.multiple_of((block_len - 1 - i) * blocks + half * ROWS, ROWS)
            g = gt_ref[pl.ds(at, ROWS), :]
            held = tuple(l * a + g for l, a in zip(wide, held))
            terms = [r * a for r, a in zip(gain, held)]
            while len(terms) > 1:
                terms = [a + b for a, b in zip(terms[::2], terms[1::2])]
            flat_ref[pl.ds(at, ROWS), :] = terms[0]
            return held

        lax.fori_loop(0, block_len, step, start, unroll=4)
    eye = identity_matrix(chans)
    for n in range(blocks):
        tile = flat_ref[pl.ds(n, block_len, stride=blocks), :].astype(jnp.bfloat16)
        out_ref[n] = flip(eye, tile).astype(jnp.bfloat16)


def mode_sums(first, blocks, x_ref, gt_ref, lam_ref, h_ref, t_ref, parts_refs):
    block_len = gt_ref.shape[0] // blocks
    lam = lam_ref[first : first + GROUP, :]
    empty = cleared(parts_refs[0], GROUP)
    wide = [spread(lam_ref, first + k) for k in range(GROUP)]
    for half in range(blocks // ROWS):

        def ahead(i, held):
            at = pl.multiple_of(i * blocks + half * ROWS, ROWS)
            g = gt_ref[pl.ds(at, ROWS), :]
            x = x_ref[pl.ds(at, ROWS), :]
            state, slope, res_sum, pole_sum = held
            slope = tuple(l * d + s for l, d, s in zip(wide, slope, state))
            state = tuple(l * s + x for l, s in zip(wide, state))
            res_sum = tuple(r + g * s for r, s in zip(res_sum, state))
            pole_sum = tuple(q + g * d for q, d in zip(pole_sum, slope))
            return (state, slope, res_sum, pole_sum)

        results = lax.fori_loop(0, block_len, ahead, (empty,) * 4, unroll=8)
        for k in range(GROUP):
            at = k * blocks + half * ROWS
            for ref, result in zip(parts_refs, results):
                ref[at : at + ROWS, :] = result[k]
    rate = log_rates(lam)
    block_step = jnp.exp(block_len * rate)
    block_slope = block_len * jnp.exp((block_len - 1) * rate)
    own = lambda ref, n: ref[pl.ds(n, GROUP, stride=blocks), :]
    of_all = lambda ref, n: ref[pl.ds(first * blocks + n, GROUP, stride=blocks), :]
    s_ref, d_ref, r_ref, q_ref = parts_refs
    state, slope, res_sum, pole_sum, total, weighted = [jnp.zeros(lam.shape, F32)] * 6
    for n in range(blocks):
        after = lam * of_all(h_ref, n)
        res_sum = res_sum + (own(r_ref, n) + state * after)
        pole_sum = pole_sum + (own(q_ref, n) + slope * after + state * of_all(t_ref, n))
        slope = block_step * slope + block_slope * state + own(d_ref, n)
        state = block_step * state + own(s_ref, n)
    for n in range(blocks - 1, -1, -1):
        weighted = block_step * (weighted + block_len * total) + of_all(t_ref, n)
        total = block_step * total + of_all(h_ref, n)
    return state, slope, res_sum, pole_sum, weighted


def sums_kernel(blocks, shifts, *refs):
    pieces, refs = refs[: len(shifts) + 1], refs[len(shifts) + 1 :]
    gt_ref, lam_ref, h_ref, t_ref, pay_ref, moved_ref, xt_ref, *parts = refs
    modes = lam_ref.shape[0]
    chips = blocks // 2
    place = lax.axis_index("chan")
    chip, core = lax.div(place, 2), lax.rem(place, 2)
    for s, ref in zip((0, *shifts), pieces):
        source = 2 * lax.rem(chip + chips - s, chips)
        moved_ref[source + core] = ref[0]
        moved_ref[source + 1 - core] = ref[1]
    flip_blocks(moved_ref, xt_ref)
    for first in range(0, modes, GROUP):
        items = mode_sums(first, blocks, xt_ref, gt_ref, lam_ref, h_ref, t_ref, parts)
        for k, item in enumerate(items):
            pay_ref[k * modes + first : k * modes + first + GROUP, :] = item


def ordered(refs, place, slots_ref):
    count = len(refs)
    for s, ref in enumerate(refs):
        slots_ref[lax.rem(place + count - s, count)] = ref[...]
    return [slots_ref[i] for i in range(count)]


def joined(lam, length, parts, heads):
    modes = lam.shape[0]
    rate = log_rates(lam)
    step = jnp.exp(length * rate)
    slope_step = length * jnp.exp((length - 1) * rate)
    state, slope, res_sum, pole_sum = [jnp.zeros(lam.shape, F32)] * 4
    tables = [[part[k * modes : (k + 1) * modes, :] for k in range(5)] for part in parts]
    for (ends, slopes, res_part, pole_part, weighted), head in zip(tables, heads):
        after = lam * head
        res_sum = res_sum + (res_part + state * after)
        pole_sum = pole_sum + (pole_part + slope * after + state * weighted)
        slope = step * slope + slope_step * state + slopes
        state = step * state + ends
    total = jnp.zeros(lam.shape, F32)
    weighted = total
    for table, head in zip(tables[::-1], heads[::-1]):
        weighted = step * (weighted + length * total) + table[4]
        total = step * total + head
    return state, slope, res_sum, pole_sum, weighted


def join_kernel(span_len, *refs):
    *parts, heads_ref, lam_ref, pay_ref, slots_ref = refs
    modes = lam_ref.shape[0]
    count = len(parts)
    place = lax.axis_index("len")
    parts = ordered(parts, lax.rem(place, count), slots_ref)
    heads = [heads_ref[place - lax.rem(place, count) + i] for i in range(count)]
    for k, item in enumerate(joined(lam_ref[...], span_len, parts, heads)):
        pay_ref[k * modes : (k + 1) * modes, :] = item


def finish_kernel(inner, span_len, *refs):
    *parts, heads_ref, lam_ref, res_ref, res_out, pole_out, slots_ref = refs
    count = len(parts)
    lam = lam_ref[...]
    step = jnp.exp(span_len * log_rates(lam))
    parts = ordered(parts, lax.div(lax.axis_index("len"), inner), slots_ref)
    heads = [
        folded(step, [heads_ref[g * inner + i] for i in range(inner)]) for g in range(count)
    ]
    _, _, res_sum, pole_sum, _ = joined(lam, inner * span_len, parts, heads)
    width = (1.0 - lam) * (1.0 + lam)
    scale = 1.0 / math.sqrt(count * inner * span_len)
    res_out[...] = res_sum * jnp.sqrt(width) * scale
    pole_out[...] = res_ref[...] * pole_sum * width * scale


def call(kernel, out_shape, in_count, scratch, name, flops, mebibytes=32):
    single = not isinstance(out_shape, (tuple, list))
    return pl.pallas_call(
        kernel,
        out_shape=out_shape,
        in_specs=[VMEM] * in_count,
        out_specs=VMEM if single else [VMEM] * len(out_shape),
        scratch_shapes=scratch,
        compiler_params=pltpu.CompilerParams(vmem_limit_bytes=mebibytes * 2**20),
        cost_estimate=pl.CostEstimate(flops=flops, bytes_accessed=2**20, transcendentals=0),
        name=name,
    )


def swap(part, axis):
    return lax.all_to_all(part, axis, split_axis=0, concat_axis=0, tiled=True)


def rotated(part, count, stride, spans):
    size = count * stride
    hop = lambda i, s: (i // size) * size + (i % size + s * stride) % size
    return [
        lax.ppermute(part, "len", [(i, hop(i, s)) for i in range(spans)]) for s in range(1, count)
    ]


def moved_pieces(part, blocks, shifts):
    chips = blocks // 2
    place = lax.axis_index("chan")
    chip, core = place // 2, place % 2
    got = lax.ppermute(part, "chan", [(i, i ^ 1) for i in range(blocks)])
    halves = [half.reshape(chips, 2, *half.shape[1:]) for half in (part, got)]
    block = lambda half, s: lax.dynamic_slice(
        half, ((chip + s) % chips, core, 0, 0), (1, 1, *half.shape[2:])
    )[0]
    at = lambda s: jnp.concatenate([block(half, s) for half in halves])
    ring = lambda s: [(i, (i + 2 * s) % blocks) for i in range(blocks)]
    return [at(0)] + [lax.ppermute(at(s), "chan", ring(s)) for s in shifts]


def body(inputs, grad_output, pole_values, residue_values):
    spans = lax.axis_size("len")
    blocks = lax.axis_size("chan")
    inner = math.isqrt(spans)
    outer = spans // inner
    chans, modes = pole_values.shape
    block_len = inputs.shape[1]
    flat = blocks * block_len
    held = modes * blocks
    work = chans * flat * modes
    shape = lambda *dims: jax.ShapeDtypeStruct(dims, F32)
    scratch = lambda *dims: pltpu.VMEM(dims, F32)
    cut = lambda part: part.reshape(blocks, chans, block_len)
    table = shape(modes, chans)
    poles = pole_values.T
    residues = residue_values.T
    moved_grads = swap(cut(grad_output), "chan")
    shifts = sorted(range(1, blocks // 2), key=lambda s: -min(s, blocks // 2 - s))
    pieces = moved_pieces(cut(inputs), blocks, shifts)
    flat_grads, ends, head = call(
        functools.partial(ends_kernel, blocks, spans),
        (shape(flat, chans), shape(held, chans), shape(spans, modes, chans)),
        2,
        [],
        "block_ends",
        2 * work,
    )(moved_grads, poles)
    heads = swap(head, "len")
    weighted = call(
        functools.partial(weighted_kernel, blocks),
        shape(held, chans),
        2,
        [],
        "weighted",
        4 * work,
    )(flat_grads, poles)
    pay = call(
        functools.partial(sums_kernel, blocks, shifts),
        shape(5 * modes, chans),
        len(pieces) + 4,
        [pltpu.VMEM((blocks, chans, block_len), jnp.bfloat16), scratch(flat, chans)]
        + [scratch(GROUP * blocks, chans)] * 4,
        "mode_sums",
        8 * work,
    )(*pieces, flat_grads, poles, ends, weighted)
    rounded = call(
        functools.partial(input_grad_kernel, blocks, spans),
        jax.ShapeDtypeStruct((blocks, chans, block_len), jnp.bfloat16),
        6,
        [scratch(held, chans), scratch(flat, chans)],
        "input_grad",
        4 * work,
    )(heads, flat_grads, poles, residues, ends, pay)
    input_grad = swap(rounded, "chan").reshape(blocks * chans, block_len)
    group_pay = call(
        functools.partial(join_kernel, flat),
        shape(5 * modes, chans),
        inner + 2,
        [scratch(inner, 5 * modes, chans)],
        "join",
        work // 100,
    )(pay, *rotated(pay, inner, 1, spans), heads, poles)
    residue_grad, pole_grad = call(
        functools.partial(finish_kernel, inner, flat),
        (table, table),
        outer + 3,
        [scratch(outer, 5 * modes, chans)],
        "finish",
        work // 100,
    )(group_pay, *rotated(group_pay, outer, inner, spans), heads, poles, residues)
    return (input_grad, residue_grad.T, pole_grad.T)


def solution(mesh):
    in_specs = (
        P(None, ("len", "chan")),
        P(None, ("len", "chan")),
        P("chan", None),
        P("chan", None),
    )
    out_specs = (P(None, ("len", "chan")), P("chan", None), P("chan", None))
    return jax.shard_map(body, mesh=mesh, in_specs=in_specs, out_specs=out_specs, check_vma=False)
```

```python
import functools
import math

import jax
import jax.numpy as jnp
from jax import lax
from jax.experimental import pallas as pl
from jax.experimental.pallas import tpu as pltpu
from jax.sharding import PartitionSpec as P

ROWS = 8
GROUP = 8
STEP = 8
F32 = jnp.float32
VMEM = pl.BlockSpec(memory_space=pltpu.VMEM)


def flip_blocks(src_ref, dst_ref):
    blocks, _, block_len = src_ref.shape
    for n in range(blocks):
        dst_ref[pl.ds(n, block_len, stride=blocks), :] = src_ref[n].astype(F32).T


def log_rates(poles):
    return jnp.log1p(-(1.0 - poles))


def cleared(ref, count):
    ref[:ROWS, :] = jnp.zeros((ROWS, ref.shape[1]), F32)
    return (ref[:ROWS, :],) * count


def block_rows(ref, n, blocks, modes):
    return ref[pl.ds(n, modes, stride=blocks), :]


def horner(rate, terms):
    total = terms[-1]
    for term in terms[-2::-1]:
        total = rate * total + term
    return total


def step_rows(ref, j, blocks, half):
    at = lambda i: pl.multiple_of((j * STEP + i) * blocks + half * ROWS, ROWS)
    return [ref[pl.ds(at(i), ROWS), :] for i in range(STEP)]


def wide_rows(table, first, count):
    return [jnp.broadcast_to(table[p : p + 1, :], (ROWS, table.shape[1])) for p in range(first, first + count)]


def put(ref, blocks, half, first, rows):
    for k, row in enumerate(rows):
        at = (first + k) * blocks + half * ROWS
        ref[at : at + ROWS, :] = row


def ends_kernel(blocks, spans, moved_ref, lam_ref, gt_ref, h_ref, head_ref):
    modes = lam_ref.shape[0]
    block_len = moved_ref.shape[2]
    steps = block_len // STEP
    flip_blocks(moved_ref, gt_ref)
    lam = lam_ref[...]
    rate = log_rates(lam)
    wide = wide_rows(lam, 0, modes)
    jump = wide_rows(jnp.exp(STEP * rate), 0, modes)
    empty = cleared(h_ref, modes)
    for half in range(blocks // ROWS):

        def back(i, held):
            j = steps - 1 - i
            g = step_rows(gt_ref, j, blocks, half)
            sums = [horner(l, g) for l in wide]
            return tuple(l * a + h for l, a, h in zip(jump, held, sums))

        put(h_ref, blocks, half, 0, lax.fori_loop(0, steps, back, empty, unroll=4))
    step = jnp.exp(block_len * rate)
    head = folded(step, [block_rows(h_ref, n, blocks, modes) for n in range(blocks)])
    for span in range(spans):
        head_ref[span] = head


def folded(step, heads):
    total = heads[-1]
    for head in heads[-2::-1]:
        total = step * total + head
    return total


def weighted_kernel(blocks, gt_ref, lam_ref, t_ref):
    modes = lam_ref.shape[0]
    block_len = gt_ref.shape[0] // blocks
    empty = cleared(t_ref, GROUP)
    for half in range(blocks // ROWS):
        for first in range(0, modes, GROUP):
            wide = wide_rows(lam_ref[...], first, GROUP)

            def back(i, held):
                at = pl.multiple_of((block_len - 1 - i) * blocks + half * ROWS, ROWS)
                g = gt_ref[pl.ds(at, ROWS), :]
                adjoint, weighted = held
                adjoint = tuple(l * a + g for l, a in zip(wide, adjoint))
                weighted = tuple(l * q + a for l, q, a in zip(wide, weighted, adjoint))
                return (adjoint, weighted)

            weighted = lax.fori_loop(0, block_len, back, (empty,) * 2, unroll=8)[1]
            for k in range(GROUP):
                at = (first + k) * blocks + half * ROWS
                t_ref[at : at + ROWS, :] = weighted[k]


def folded_after(step, heads, place):
    total = jnp.zeros(step.shape, F32)
    for i in range(len(heads) - 1, 0, -1):
        total = jnp.where(i > place, step * total + heads[i], total)
    return total


def input_grad_kernel(
    blocks, spans, heads_ref, gt_ref, lam_ref, res_ref, h_ref, _, out_ref, next_ref, flat_ref
):
    modes, chans = lam_ref.shape
    block_len = gt_ref.shape[0] // blocks
    rate = log_rates(lam_ref[...])
    block_step = jnp.exp(block_len * rate)
    span_step = jnp.exp((blocks * block_len) * rate)
    total = folded_after(span_step, [heads_ref[i] for i in range(spans)], lax.axis_index("len"))
    for n in range(blocks - 1, -1, -1):
        next_ref[pl.ds(n, modes, stride=blocks), :] = total
        total = block_step * total + block_rows(h_ref, n, blocks, modes)
    for half in range(blocks // ROWS):
        wide = wide_rows(lam_ref[...], 0, modes)
        gain = wide_rows(res_ref[...], 0, modes)
        start = tuple(
            next_ref[p * blocks + half * ROWS : p * blocks + half * ROWS + ROWS, :]
            for p in range(modes)
        )

        def step(i, held):
            at = pl.multiple_of((block_len - 1 - i) * blocks + half * ROWS, ROWS)
            g = gt_ref[pl.ds(at, ROWS), :]
            held = tuple(l * a + g for l, a in zip(wide, held))
            terms = [r * a for r, a in zip(gain, held)]
            while len(terms) > 1:
                terms = [a + b for a, b in zip(terms[::2], terms[1::2])]
            flat_ref[pl.ds(at, ROWS), :] = terms[0]
            return held

        lax.fori_loop(0, block_len, step, start, unroll=4)
    for n in range(blocks):
        out_ref[n] = flat_ref[pl.ds(n, block_len, stride=blocks), :].T.astype(jnp.bfloat16)


def mode_sums(first, blocks, x_ref, gt_ref, lam_ref, h_ref, t_ref, parts_refs):
    block_len = gt_ref.shape[0] // blocks
    lam = lam_ref[first : first + GROUP, :]
    empty = cleared(parts_refs[0], GROUP)
    wide = wide_rows(lam, 0, GROUP)
    for half in range(blocks // ROWS):

        def ahead(i, held):
            at = pl.multiple_of(i * blocks + half * ROWS, ROWS)
            g = gt_ref[pl.ds(at, ROWS), :]
            x = x_ref[pl.ds(at, ROWS), :]
            state, slope, res_sum, pole_sum = held
            slope = tuple(l * d + s for l, d, s in zip(wide, slope, state))
            state = tuple(l * s + x for l, s in zip(wide, state))
            res_sum = tuple(r + g * s for r, s in zip(res_sum, state))
            pole_sum = tuple(q + g * d for q, d in zip(pole_sum, slope))
            return (state, slope, res_sum, pole_sum)

        results = lax.fori_loop(0, block_len, ahead, (empty,) * 4, unroll=8)
        for k in range(GROUP):
            at = k * blocks + half * ROWS
            for ref, result in zip(parts_refs, results):
                ref[at : at + ROWS, :] = result[k]
    rate = log_rates(lam)
    block_step = jnp.exp(block_len * rate)
    block_slope = block_len * jnp.exp((block_len - 1) * rate)
    own = lambda ref, n: ref[pl.ds(n, GROUP, stride=blocks), :]
    of_all = lambda ref, n: ref[pl.ds(first * blocks + n, GROUP, stride=blocks), :]
    s_ref, d_ref, r_ref, q_ref = parts_refs
    state, slope, res_sum, pole_sum, total, weighted = [jnp.zeros(lam.shape, F32)] * 6
    for n in range(blocks):
        after = lam * of_all(h_ref, n)
        res_sum = res_sum + (own(r_ref, n) + state * after)
        pole_sum = pole_sum + (own(q_ref, n) + slope * after + state * of_all(t_ref, n))
        slope = block_step * slope + block_slope * state + own(d_ref, n)
        state = block_step * state + own(s_ref, n)
    for n in range(blocks - 1, -1, -1):
        weighted = block_step * (weighted + block_len * total) + of_all(t_ref, n)
        total = block_step * total + of_all(h_ref, n)
    return state, slope, res_sum, pole_sum, weighted


def sums_kernel(blocks, shifts, *refs):
    pieces, refs = refs[: len(shifts) + 1], refs[len(shifts) + 1 :]
    gt_ref, lam_ref, h_ref, t_ref, pay_ref, moved_ref, xt_ref, *parts = refs
    modes = lam_ref.shape[0]
    chips = blocks // 2
    place = lax.axis_index("chan")
    chip, core = lax.div(place, 2), lax.rem(place, 2)
    for s, ref in zip((0, *shifts), pieces):
        source = 2 * lax.rem(chip + chips - s, chips)
        moved_ref[source + core] = ref[0]
        moved_ref[source + 1 - core] = ref[1]
    flip_blocks(moved_ref, xt_ref)
    for first in range(0, modes, GROUP):
        items = mode_sums(first, blocks, xt_ref, gt_ref, lam_ref, h_ref, t_ref, parts)
        for k, item in enumerate(items):
            pay_ref[k * modes + first : k * modes + first + GROUP, :] = item


def ordered(refs, place, slots_ref):
    count = len(refs)
    for s, ref in enumerate(refs):
        slots_ref[lax.rem(place + count - s, count)] = ref[...]
    return [slots_ref[i] for i in range(count)]


def joined(lam, length, parts, heads):
    modes = lam.shape[0]
    rate = log_rates(lam)
    step = jnp.exp(length * rate)
    slope_step = length * jnp.exp((length - 1) * rate)
    state, slope, res_sum, pole_sum = [jnp.zeros(lam.shape, F32)] * 4
    tables = [[part[k * modes : (k + 1) * modes, :] for k in range(5)] for part in parts]
    for (ends, slopes, res_part, pole_part, weighted), head in zip(tables, heads):
        after = lam * head
        res_sum = res_sum + (res_part + state * after)
        pole_sum = pole_sum + (pole_part + slope * after + state * weighted)
        slope = step * slope + slope_step * state + slopes
        state = step * state + ends
    total = jnp.zeros(lam.shape, F32)
    weighted = total
    for table, head in zip(tables[::-1], heads[::-1]):
        weighted = step * (weighted + length * total) + table[4]
        total = step * total + head
    return state, slope, res_sum, pole_sum, weighted


def join_kernel(span_len, *refs):
    *parts, heads_ref, lam_ref, pay_ref, slots_ref = refs
    modes = lam_ref.shape[0]
    count = len(parts)
    place = lax.axis_index("len")
    parts = ordered(parts, lax.rem(place, count), slots_ref)
    heads = [heads_ref[place - lax.rem(place, count) + i] for i in range(count)]
    for k, item in enumerate(joined(lam_ref[...], span_len, parts, heads)):
        pay_ref[k * modes : (k + 1) * modes, :] = item


def finish_kernel(inner, span_len, *refs):
    *parts, heads_ref, lam_ref, res_ref, res_out, pole_out, slots_ref = refs
    count = len(parts)
    lam = lam_ref[...]
    step = jnp.exp(span_len * log_rates(lam))
    parts = ordered(parts, lax.div(lax.axis_index("len"), inner), slots_ref)
    heads = [
        folded(step, [heads_ref[g * inner + i] for i in range(inner)]) for g in range(count)
    ]
    _, _, res_sum, pole_sum, _ = joined(lam, inner * span_len, parts, heads)
    width = (1.0 - lam) * (1.0 + lam)
    scale = 1.0 / math.sqrt(count * inner * span_len)
    res_out[...] = res_sum * jnp.sqrt(width) * scale
    pole_out[...] = res_ref[...] * pole_sum * width * scale


def call(kernel, out_shape, in_count, scratch, name, flops, mebibytes=32):
    single = not isinstance(out_shape, (tuple, list))
    return pl.pallas_call(
        kernel,
        out_shape=out_shape,
        in_specs=[VMEM] * in_count,
        out_specs=VMEM if single else [VMEM] * len(out_shape),
        scratch_shapes=scratch,
        compiler_params=pltpu.CompilerParams(vmem_limit_bytes=mebibytes * 2**20),
        cost_estimate=pl.CostEstimate(flops=flops, bytes_accessed=2**20, transcendentals=0),
        name=name,
    )


def swap(part, axis):
    return lax.all_to_all(part, axis, split_axis=0, concat_axis=0, tiled=True)


def rotated(part, count, stride, spans):
    size = count * stride
    hop = lambda i, s: (i // size) * size + (i % size + s * stride) % size
    return [
        lax.ppermute(part, "len", [(i, hop(i, s)) for i in range(spans)]) for s in range(1, count)
    ]


def moved_pieces(part, blocks, shifts):
    chips = blocks // 2
    place = lax.axis_index("chan")
    chip, core = place // 2, place % 2
    got = lax.ppermute(part, "chan", [(i, i ^ 1) for i in range(blocks)])
    halves = [half.reshape(chips, 2, *half.shape[1:]) for half in (part, got)]
    block = lambda half, s: lax.dynamic_slice(
        half, ((chip + s) % chips, core, 0, 0), (1, 1, *half.shape[2:])
    )[0]
    at = lambda s: jnp.concatenate([block(half, s) for half in halves])
    ring = lambda s: [(i, (i + 2 * s) % blocks) for i in range(blocks)]
    return [at(0)] + [lax.ppermute(at(s), "chan", ring(s)) for s in shifts]


def body(inputs, grad_output, pole_values, residue_values):
    spans = lax.axis_size("len")
    blocks = lax.axis_size("chan")
    inner = math.isqrt(spans)
    outer = spans // inner
    chans, modes = pole_values.shape
    block_len = inputs.shape[1]
    flat = blocks * block_len
    held = modes * blocks
    work = chans * flat * modes
    shape = lambda *dims: jax.ShapeDtypeStruct(dims, F32)
    scratch = lambda *dims: pltpu.VMEM(dims, F32)
    cut = lambda part: part.reshape(blocks, chans, block_len)
    table = shape(modes, chans)
    poles = pole_values.T
    residues = residue_values.T
    moved_grads = swap(cut(grad_output), "chan")
    shifts = sorted(range(1, blocks // 2), key=lambda s: -min(s, blocks // 2 - s))
    pieces = moved_pieces(cut(inputs), blocks, shifts)
    flat_grads, ends, head = call(
        functools.partial(ends_kernel, blocks, spans),
        (shape(flat, chans), shape(held, chans), shape(spans, modes, chans)),
        2,
        [],
        "block_ends",
        2 * work,
    )(moved_grads, poles)
    heads = swap(head, "len")
    weighted = call(
        functools.partial(weighted_kernel, blocks),
        shape(held, chans),
        2,
        [],
        "weighted",
        4 * work,
    )(flat_grads, poles)
    pay = call(
        functools.partial(sums_kernel, blocks, shifts),
        shape(5 * modes, chans),
        len(pieces) + 4,
        [pltpu.VMEM((blocks, chans, block_len), jnp.bfloat16), scratch(flat, chans)]
        + [scratch(GROUP * blocks, chans)] * 4,
        "mode_sums",
        8 * work,
    )(*pieces, flat_grads, poles, ends, weighted)
    rounded = call(
        functools.partial(input_grad_kernel, blocks, spans),
        jax.ShapeDtypeStruct((blocks, chans, block_len), jnp.bfloat16),
        6,
        [scratch(held, chans), scratch(flat, chans)],
        "input_grad",
        4 * work,
    )(heads, flat_grads, poles, residues, ends, pay)
    input_grad = swap(rounded, "chan").reshape(blocks * chans, block_len)
    group_pay = call(
        functools.partial(join_kernel, flat),
        shape(5 * modes, chans),
        inner + 2,
        [scratch(inner, 5 * modes, chans)],
        "join",
        work // 100,
    )(pay, *rotated(pay, inner, 1, spans), heads, poles)
    residue_grad, pole_grad = call(
        functools.partial(finish_kernel, inner, flat),
        (table, table),
        outer + 3,
        [scratch(outer, 5 * modes, chans)],
        "finish",
        work // 100,
    )(group_pay, *rotated(group_pay, outer, inner, spans), heads, poles, residues)
    return (input_grad, residue_grad.T, pole_grad.T)


def solution(mesh):
    in_specs = (
        P(None, ("len", "chan")),
        P(None, ("len", "chan")),
        P("chan", None),
        P("chan", None),
    )
    out_specs = (P(None, ("len", "chan")), P("chan", None), P("chan", None))
    return jax.shard_map(body, mesh=mesh, in_specs=in_specs, out_specs=out_specs, check_vma=False)
```

```python
import functools
import math

import jax
import jax.numpy as jnp
from jax import lax
from jax.experimental import pallas as pl
from jax.experimental.pallas import tpu as pltpu
from jax.sharding import PartitionSpec as P

ROWS = 8
GROUP = 8
STEP = 8
F32 = jnp.float32
VMEM = pl.BlockSpec(memory_space=pltpu.VMEM)


def flip_blocks(src_ref, dst_ref):
    blocks, _, block_len = src_ref.shape
    for n in range(blocks):
        dst_ref[pl.ds(n, block_len, stride=blocks), :] = src_ref[n].astype(F32).T


def log_rates(poles):
    return jnp.log1p(-(1.0 - poles))


def cleared(ref, count):
    ref[:ROWS, :] = jnp.zeros((ROWS, ref.shape[1]), F32)
    return (ref[:ROWS, :],) * count


def block_rows(ref, n, blocks, modes):
    return ref[pl.ds(n, modes, stride=blocks), :]


def horner(rate, terms):
    total = terms[-1]
    for term in terms[-2::-1]:
        total = rate * total + term
    return total


def step_rows(ref, j, blocks, half):
    at = lambda i: pl.multiple_of((j * STEP + i) * blocks + half * ROWS, ROWS)
    return [ref[pl.ds(at(i), ROWS), :] for i in range(STEP)]


def slot(j, blocks, half, modes, p):
    at = ((j * (blocks // ROWS) + half) * modes + p) * ROWS
    return pl.ds(pl.multiple_of(at, ROWS), ROWS)


def wide_rows(table, first, count):
    return [jnp.broadcast_to(table[p : p + 1, :], (ROWS, table.shape[1])) for p in range(first, first + count)]


def put(ref, blocks, half, first, rows):
    for k, row in enumerate(rows):
        at = (first + k) * blocks + half * ROWS
        ref[at : at + ROWS, :] = row


def ends_kernel(blocks, spans, moved_ref, lam_ref, gt_ref, h_ref, head_ref):
    modes = lam_ref.shape[0]
    block_len = moved_ref.shape[2]
    steps = block_len // STEP
    flip_blocks(moved_ref, gt_ref)
    lam = lam_ref[...]
    rate = log_rates(lam)
    wide = wide_rows(lam, 0, modes)
    jump = wide_rows(jnp.exp(STEP * rate), 0, modes)
    empty = cleared(h_ref, modes)
    for half in range(blocks // ROWS):

        def back(i, held):
            j = steps - 1 - i
            g = step_rows(gt_ref, j, blocks, half)
            sums = [horner(l, g) for l in wide]
            return tuple(l * a + h for l, a, h in zip(jump, held, sums))

        put(h_ref, blocks, half, 0, lax.fori_loop(0, steps, back, empty, unroll=8))
    step = jnp.exp(block_len * rate)
    head = folded(step, [block_rows(h_ref, n, blocks, modes) for n in range(blocks)])
    for span in range(spans):
        head_ref[span] = head


def folded(step, heads):
    total = heads[-1]
    for head in heads[-2::-1]:
        total = step * total + head
    return total


def weighted_kernel(blocks, gt_ref, lam_ref, sub_ref, sub_t_ref, t_ref):
    modes = lam_ref.shape[0]
    steps = gt_ref.shape[0] // blocks // STEP
    lam = lam_ref[...]
    jumps = jnp.exp(STEP * log_rates(lam))
    empty = cleared(t_ref, GROUP)
    for first in range(0, modes, GROUP):
        wide = wide_rows(lam, first, GROUP)
        jump = wide_rows(jumps, first, GROUP)
        for half in range(blocks // ROWS):

            def back(i, held):
                j = steps - 1 - i
                g = step_rows(gt_ref, j, blocks, half)
                scaled = [(k + 1.0) * row for k, row in enumerate(g)]
                adjoint, weighted = held
                after, total = [], []
                for k in range(GROUP):
                    rows = slot(j, blocks, half, modes, first + k)
                    head = horner(wide[k], g)
                    part = horner(wide[k], scaled)
                    sub_ref[rows, :] = head
                    sub_t_ref[rows, :] = part
                    total.append(jump[k] * (weighted[k] + STEP * adjoint[k]) + part)
                    after.append(jump[k] * adjoint[k] + head)
                return (tuple(after), tuple(total))

            weighted = lax.fori_loop(0, steps, back, (empty,) * 2, unroll=4)[1]
            put(t_ref, blocks, half, first, weighted)


def folded_after(step, heads, place):
    total = jnp.zeros(step.shape, F32)
    for i in range(len(heads) - 1, 0, -1):
        total = jnp.where(i > place, step * total + heads[i], total)
    return total


def input_grad_kernel(
    blocks, spans, heads_ref, gt_ref, lam_ref, res_ref, h_ref, _, out_ref, next_ref, flat_ref
):
    modes, chans = lam_ref.shape
    block_len = gt_ref.shape[0] // blocks
    rate = log_rates(lam_ref[...])
    block_step = jnp.exp(block_len * rate)
    span_step = jnp.exp((blocks * block_len) * rate)
    total = folded_after(span_step, [heads_ref[i] for i in range(spans)], lax.axis_index("len"))
    for n in range(blocks - 1, -1, -1):
        next_ref[pl.ds(n, modes, stride=blocks), :] = total
        total = block_step * total + block_rows(h_ref, n, blocks, modes)
    for half in range(blocks // ROWS):
        wide = wide_rows(lam_ref[...], 0, modes)
        gain = wide_rows(res_ref[...], 0, modes)
        start = tuple(
            next_ref[p * blocks + half * ROWS : p * blocks + half * ROWS + ROWS, :]
            for p in range(modes)
        )

        def step(i, held):
            at = pl.multiple_of((block_len - 1 - i) * blocks + half * ROWS, ROWS)
            g = gt_ref[pl.ds(at, ROWS), :]
            held = tuple(l * a + g for l, a in zip(wide, held))
            terms = [r * a for r, a in zip(gain, held)]
            while len(terms) > 1:
                terms = [a + b for a, b in zip(terms[::2], terms[1::2])]
            flat_ref[pl.ds(at, ROWS), :] = terms[0]
            return held

        lax.fori_loop(0, block_len, step, start, unroll=8)
    for n in range(blocks):
        out_ref[n] = flat_ref[pl.ds(n, block_len, stride=blocks), :].T.astype(jnp.bfloat16)


def lag_sums(blocks, steps, x_ref, gt_ref, zero):
    lags = (zero,) * STEP
    for half in range(blocks // ROWS):

        def ahead(j, held):
            g = step_rows(gt_ref, j, blocks, half)
            x = step_rows(x_ref, j, blocks, half)
            return tuple(
                total + sum(g[i] * x[i - k] for i in range(k, STEP)) for k, total in enumerate(held)
            )

        lags = lax.fori_loop(0, steps, ahead, lags, unroll=8)
    return [jnp.sum(lag, axis=0, keepdims=True) for lag in lags]


def mode_sums(first, blocks, lags, x_ref, gt_ref, subs, lam_ref, h_ref, t_ref, parts_refs):
    modes = lam_ref.shape[0]
    block_len = gt_ref.shape[0] // blocks
    steps = block_len // STEP
    sub_ref, sub_t_ref = subs
    lam = lam_ref[first : first + GROUP, :]
    rate = log_rates(lam)
    empty = cleared(parts_refs[0], GROUP)
    wide = wide_rows(lam, 0, GROUP)
    jump = wide_rows(jnp.exp(STEP * rate), 0, GROUP)
    jump_slope = wide_rows(STEP * jnp.exp((STEP - 1) * rate), 0, GROUP)
    for half in range(blocks // ROWS):

        def ahead(j, held):
            x = step_rows(x_ref, j, blocks, half)[::-1]
            scaled = [k * x[k] for k in range(1, STEP)]
            state, slope, res_sum, pole_sum = [list(part) for part in held]
            for k in range(GROUP):
                rows = slot(j, blocks, half, modes, first + k)
                after = wide[k] * sub_ref[rows, :]
                res_sum[k] = res_sum[k] + state[k] * after
                pole_sum[k] = pole_sum[k] + (slope[k] * after + state[k] * sub_t_ref[rows, :])
                grown = jump[k] * slope[k] + jump_slope[k] * state[k]
                slope[k] = grown + horner(wide[k], scaled)
                state[k] = jump[k] * state[k] + horner(wide[k], x)
            return (tuple(state), tuple(slope), tuple(res_sum), tuple(pole_sum))

        results = lax.fori_loop(0, steps, ahead, (empty,) * 4, unroll=8)
        for ref, result in zip(parts_refs, results):
            put(ref, blocks, half, 0, result)
    block_step = jnp.exp(block_len * rate)
    block_slope = block_len * jnp.exp((block_len - 1) * rate)
    own = lambda ref, n: ref[pl.ds(n, GROUP, stride=blocks), :]
    of_all = lambda ref, n: ref[pl.ds(first * blocks + n, GROUP, stride=blocks), :]
    s_ref, d_ref, r_ref, q_ref = parts_refs
    state, slope, total, weighted = [jnp.zeros(lam.shape, F32)] * 4
    res_sum = horner(lam, lags)
    pole_sum = horner(lam, [k * lags[k] for k in range(1, STEP)])
    for n in range(blocks):
        after = lam * of_all(h_ref, n)
        res_sum = res_sum + (own(r_ref, n) + state * after)
        pole_sum = pole_sum + (own(q_ref, n) + slope * after + state * of_all(t_ref, n))
        slope = block_step * slope + block_slope * state + own(d_ref, n)
        state = block_step * state + own(s_ref, n)
    for n in range(blocks - 1, -1, -1):
        weighted = block_step * (weighted + block_len * total) + of_all(t_ref, n)
        total = block_step * total + of_all(h_ref, n)
    return state, slope, res_sum, pole_sum, weighted


def sums_kernel(blocks, shifts, *refs):
    pieces, refs = refs[: len(shifts) + 1], refs[len(shifts) + 1 :]
    gt_ref, sub_ref, sub_t_ref, lam_ref, h_ref, t_ref, pay_ref, moved_ref, xt_ref, *parts = refs
    modes = lam_ref.shape[0]
    chips = blocks // 2
    place = lax.axis_index("chan")
    chip, core = lax.div(place, 2), lax.rem(place, 2)
    for s, ref in zip((0, *shifts), pieces):
        source = 2 * lax.rem(chip + chips - s, chips)
        moved_ref[source + core] = ref[0]
        moved_ref[source + 1 - core] = ref[1]
    flip_blocks(moved_ref, xt_ref)
    steps = gt_ref.shape[0] // blocks // STEP
    lags = lag_sums(blocks, steps, xt_ref, gt_ref, cleared(parts[0], 1)[0])
    subs = (sub_ref, sub_t_ref)
    for first in range(0, modes, GROUP):
        items = mode_sums(first, blocks, lags, xt_ref, gt_ref, subs, lam_ref, h_ref, t_ref, parts)
        for k, item in enumerate(items):
            pay_ref[k * modes + first : k * modes + first + GROUP, :] = item


def ordered(refs, place, slots_ref):
    count = len(refs)
    for s, ref in enumerate(refs):
        slots_ref[lax.rem(place + count - s, count)] = ref[...]
    return [slots_ref[i] for i in range(count)]


def joined(lam, length, parts, heads):
    modes = lam.shape[0]
    rate = log_rates(lam)
    step = jnp.exp(length * rate)
    slope_step = length * jnp.exp((length - 1) * rate)
    state, slope, res_sum, pole_sum = [jnp.zeros(lam.shape, F32)] * 4
    tables = [[part[k * modes : (k + 1) * modes, :] for k in range(5)] for part in parts]
    for (ends, slopes, res_part, pole_part, weighted), head in zip(tables, heads):
        after = lam * head
        res_sum = res_sum + (res_part + state * after)
        pole_sum = pole_sum + (pole_part + slope * after + state * weighted)
        slope = step * slope + slope_step * state + slopes
        state = step * state + ends
    total = jnp.zeros(lam.shape, F32)
    weighted = total
    for table, head in zip(tables[::-1], heads[::-1]):
        weighted = step * (weighted + length * total) + table[4]
        total = step * total + head
    return state, slope, res_sum, pole_sum, weighted


def join_kernel(span_len, *refs):
    *parts, heads_ref, lam_ref, pay_ref, slots_ref = refs
    modes = lam_ref.shape[0]
    count = len(parts)
    place = lax.axis_index("len")
    parts = ordered(parts, lax.rem(place, count), slots_ref)
    heads = [heads_ref[place - lax.rem(place, count) + i] for i in range(count)]
    for k, item in enumerate(joined(lam_ref[...], span_len, parts, heads)):
        pay_ref[k * modes : (k + 1) * modes, :] = item


def finish_kernel(inner, span_len, *refs):
    *parts, heads_ref, lam_ref, res_ref, res_out, pole_out, slots_ref = refs
    count = len(parts)
    lam = lam_ref[...]
    step = jnp.exp(span_len * log_rates(lam))
    parts = ordered(parts, lax.div(lax.axis_index("len"), inner), slots_ref)
    heads = [
        folded(step, [heads_ref[g * inner + i] for i in range(inner)]) for g in range(count)
    ]
    _, _, res_sum, pole_sum, _ = joined(lam, inner * span_len, parts, heads)
    width = (1.0 - lam) * (1.0 + lam)
    scale = 1.0 / math.sqrt(count * inner * span_len)
    res_out[...] = res_sum * jnp.sqrt(width) * scale
    pole_out[...] = res_ref[...] * pole_sum * width * scale


def call(kernel, out_shape, in_count, scratch, name, flops, mebibytes=32):
    single = not isinstance(out_shape, (tuple, list))
    return pl.pallas_call(
        kernel,
        out_shape=out_shape,
        in_specs=[VMEM] * in_count,
        out_specs=VMEM if single else [VMEM] * len(out_shape),
        scratch_shapes=scratch,
        compiler_params=pltpu.CompilerParams(vmem_limit_bytes=mebibytes * 2**20),
        cost_estimate=pl.CostEstimate(flops=flops, bytes_accessed=2**20, transcendentals=0),
        name=name,
    )


def swap(part, axis):
    return lax.all_to_all(part, axis, split_axis=0, concat_axis=0, tiled=True)


def rotated(part, count, stride, spans):
    size = count * stride
    hop = lambda i, s: (i // size) * size + (i % size + s * stride) % size
    return [
        lax.ppermute(part, "len", [(i, hop(i, s)) for i in range(spans)]) for s in range(1, count)
    ]


def moved_pieces(part, blocks, shifts):
    chips = blocks // 2
    place = lax.axis_index("chan")
    chip, core = place // 2, place % 2
    got = lax.ppermute(part, "chan", [(i, i ^ 1) for i in range(blocks)])
    halves = [half.reshape(chips, 2, *half.shape[1:]) for half in (part, got)]
    block = lambda half, s: lax.dynamic_slice(
        half, ((chip + s) % chips, core, 0, 0), (1, 1, *half.shape[2:])
    )[0]
    at = lambda s: jnp.concatenate([block(half, s) for half in halves])
    ring = lambda s: [(i, (i + 2 * s) % blocks) for i in range(blocks)]
    return [at(0)] + [lax.ppermute(at(s), "chan", ring(s)) for s in shifts]


def body(inputs, grad_output, pole_values, residue_values):
    spans = lax.axis_size("len")
    blocks = lax.axis_size("chan")
    inner = math.isqrt(spans)
    outer = spans // inner
    chans, modes = pole_values.shape
    block_len = inputs.shape[1]
    flat = blocks * block_len
    held = modes * blocks
    work = chans * flat * modes
    shape = lambda *dims: jax.ShapeDtypeStruct(dims, F32)
    scratch = lambda *dims: pltpu.VMEM(dims, F32)
    cut = lambda part: part.reshape(blocks, chans, block_len)
    table = shape(modes, chans)
    poles = pole_values.T
    residues = residue_values.T
    moved_grads = swap(cut(grad_output), "chan")
    shifts = sorted(range(1, blocks // 2), key=lambda s: -min(s, blocks // 2 - s))
    pieces = moved_pieces(cut(inputs), blocks, shifts)
    flat_grads, ends, head = call(
        functools.partial(ends_kernel, blocks, spans),
        (shape(flat, chans), shape(held, chans), shape(spans, modes, chans)),
        2,
        [],
        "block_ends",
        2 * work,
    )(moved_grads, poles)
    heads = swap(head, "len")
    subs = shape(held * block_len // STEP, chans)
    sub_heads, sub_weighted, weighted = call(
        functools.partial(weighted_kernel, blocks),
        (subs, subs, shape(held, chans)),
        2,
        [],
        "weighted",
        4 * work,
    )(flat_grads, poles)
    pay = call(
        functools.partial(sums_kernel, blocks, shifts),
        shape(5 * modes, chans),
        len(pieces) + 6,
        [pltpu.VMEM((blocks, chans, block_len), jnp.bfloat16), scratch(flat, chans)]
        + [scratch(GROUP * blocks, chans)] * 4,
        "mode_sums",
        8 * work,
    )(*pieces, flat_grads, sub_heads, sub_weighted, poles, ends, weighted)
    rounded = call(
        functools.partial(input_grad_kernel, blocks, spans),
        jax.ShapeDtypeStruct((blocks, chans, block_len), jnp.bfloat16),
        6,
        [scratch(held, chans), scratch(flat, chans)],
        "input_grad",
        4 * work,
    )(heads, flat_grads, poles, residues, ends, pay)
    input_grad = swap(rounded, "chan").reshape(blocks * chans, block_len)
    group_pay = call(
        functools.partial(join_kernel, flat),
        shape(5 * modes, chans),
        inner + 2,
        [scratch(inner, 5 * modes, chans)],
        "join",
        work // 100,
    )(pay, *rotated(pay, inner, 1, spans), heads, poles)
    residue_grad, pole_grad = call(
        functools.partial(finish_kernel, inner, flat),
        (table, table),
        outer + 3,
        [scratch(outer, 5 * modes, chans)],
        "finish",
        work // 100,
    )(group_pay, *rotated(group_pay, outer, inner, spans), heads, poles, residues)
    return (input_grad, residue_grad.T, pole_grad.T)


def solution(mesh):
    in_specs = (
        P(None, ("len", "chan")),
        P(None, ("len", "chan")),
        P("chan", None),
        P("chan", None),
    )
    out_specs = (P(None, ("len", "chan")), P("chan", None), P("chan", None))
    return jax.shard_map(body, mesh=mesh, in_specs=in_specs, out_specs=out_specs, check_vma=False)
```

```python
import functools
import math

import jax
import jax.numpy as jnp
from jax import lax
from jax.experimental import pallas as pl
from jax.experimental.pallas import tpu as pltpu
from jax.sharding import PartitionSpec as P

ROWS = 8
GROUP = 8
STEP = 8
F32 = jnp.float32
VMEM = pl.BlockSpec(memory_space=pltpu.VMEM)


def flip_blocks(src_ref, dst_ref):
    blocks, _, block_len = src_ref.shape
    for n in range(blocks):
        dst_ref[pl.ds(n, block_len, stride=blocks), :] = src_ref[n].astype(F32).T


def log_rates(poles):
    return jnp.log1p(-(1.0 - poles))


def cleared(ref, count):
    ref[:ROWS, :] = jnp.zeros((ROWS, ref.shape[1]), F32)
    return (ref[:ROWS, :],) * count


def block_rows(ref, n, blocks, modes):
    return ref[pl.ds(n, modes, stride=blocks), :]


def horner(rate, terms):
    total = terms[-1]
    for term in terms[-2::-1]:
        total = rate * total + term
    return total


def step_rows(ref, j, blocks, half):
    if ref.dtype == F32:
        at = lambda i: pl.multiple_of((j * STEP + i) * blocks + half * ROWS, ROWS)
        return [ref[pl.ds(at(i), ROWS), :] for i in range(STEP)]
    at = lambda i: pl.multiple_of((j * STEP + i) * blocks, blocks)
    rows = slice(half * ROWS, (half + 1) * ROWS)
    return [ref[pl.ds(at(i), blocks), :].astype(F32)[rows, :] for i in range(STEP)]


def slot(j, blocks, half, modes, p):
    at = ((j * (blocks // ROWS) + half) * modes + p) * ROWS
    return pl.ds(pl.multiple_of(at, ROWS), ROWS)


def wide_rows(table, first, count):
    return [jnp.broadcast_to(table[p : p + 1, :], (ROWS, table.shape[1])) for p in range(first, first + count)]


def put(ref, blocks, half, first, rows):
    for k, row in enumerate(rows):
        at = (first + k) * blocks + half * ROWS
        ref[at : at + ROWS, :] = row


def ends_kernel(blocks, spans, moved_ref, lam_ref, gt_ref, h_ref, head_ref, wide_ref):
    modes = lam_ref.shape[0]
    block_len = moved_ref.shape[2]
    steps = block_len // STEP
    flip_blocks(moved_ref, wide_ref)
    gt_ref[...] = wide_ref[...].astype(jnp.bfloat16)
    lam = lam_ref[...]
    rate = log_rates(lam)
    wide = wide_rows(lam, 0, modes)
    jump = wide_rows(jnp.exp(STEP * rate), 0, modes)
    empty = cleared(h_ref, modes)
    for half in range(blocks // ROWS):

        def back(i, held):
            j = steps - 1 - i
            g = step_rows(wide_ref, j, blocks, half)
            sums = [horner(l, g) for l in wide]
            return tuple(l * a + h for l, a, h in zip(jump, held, sums))

        put(h_ref, blocks, half, 0, lax.fori_loop(0, steps, back, empty, unroll=8))
    step = jnp.exp(block_len * rate)
    head = folded(step, [block_rows(h_ref, n, blocks, modes) for n in range(blocks)])
    for span in range(spans):
        head_ref[span] = head


def folded(step, heads):
    total = heads[-1]
    for head in heads[-2::-1]:
        total = step * total + head
    return total


def weighted_kernel(blocks, gt_ref, lam_ref, sub_ref, sub_t_ref, t_ref):
    modes = lam_ref.shape[0]
    steps = gt_ref.shape[0] // blocks // STEP
    lam = lam_ref[...]
    jumps = jnp.exp(STEP * log_rates(lam))
    empty = cleared(t_ref, GROUP)
    for first in range(0, modes, GROUP):
        wide = wide_rows(lam, first, GROUP)
        jump = wide_rows(jumps, first, GROUP)
        for half in range(blocks // ROWS):

            def back(i, held):
                j = steps - 1 - i
                g = step_rows(gt_ref, j, blocks, half)
                scaled = [(k + 1.0) * row for k, row in enumerate(g)]
                adjoint, weighted = held
                after, total = [], []
                for k in range(GROUP):
                    rows = slot(j, blocks, half, modes, first + k)
                    head = horner(wide[k], g)
                    part = horner(wide[k], scaled)
                    sub_ref[rows, :] = head
                    sub_t_ref[rows, :] = part
                    total.append(jump[k] * (weighted[k] + STEP * adjoint[k]) + part)
                    after.append(jump[k] * adjoint[k] + head)
                return (tuple(after), tuple(total))

            weighted = lax.fori_loop(0, steps, back, (empty,) * 2, unroll=4)[1]
            put(t_ref, blocks, half, first, weighted)


def folded_after(step, heads, place):
    total = jnp.zeros(step.shape, F32)
    for i in range(len(heads) - 1, 0, -1):
        total = jnp.where(i > place, step * total + heads[i], total)
    return total


def input_grad_kernel(
    blocks, spans, heads_ref, gt_ref, sub_ref, lam_ref, res_ref, h_ref, _, out_ref, next_ref, flat_ref
):
    modes = lam_ref.shape[0]
    block_len = gt_ref.shape[0] // blocks
    steps = block_len // STEP
    lam = lam_ref[...]
    res = res_ref[...]
    rate = log_rates(lam)
    block_step = jnp.exp(block_len * rate)
    span_step = jnp.exp((blocks * block_len) * rate)
    total = folded_after(span_step, [heads_ref[i] for i in range(spans)], lax.axis_index("len"))
    for n in range(blocks - 1, -1, -1):
        next_ref[pl.ds(n, modes, stride=blocks), :] = total
        total = block_step * total + block_rows(h_ref, n, blocks, modes)
    taps, power = [], res
    for _ in range(STEP):
        taps.append(jnp.broadcast_to(jnp.sum(power, axis=0, keepdims=True), (ROWS, lam.shape[1])))
        power = power * lam
    wide = wide_rows(lam, 0, modes)
    jump = wide_rows(jnp.exp(STEP * rate), 0, modes)
    gain = wide_rows(res, 0, modes)
    for half in range(blocks // ROWS):
        start = tuple(
            next_ref[p * blocks + half * ROWS : p * blocks + half * ROWS + ROWS, :]
            for p in range(modes)
        )

        def back(i, held):
            j = steps - 1 - i
            g = step_rows(gt_ref, j, blocks, half)
            outs = [sum(taps[k] * g[at + k] for k in range(STEP - at)) for at in range(STEP)]
            after = []
            for p in range(modes):
                term = gain[p] * held[p]
                for at in range(STEP - 1, -1, -1):
                    term = wide[p] * term
                    outs[at] = outs[at] + term
                after.append(jump[p] * held[p] + sub_ref[slot(j, blocks, half, modes, p), :])
            for at in range(STEP):
                rows = pl.multiple_of((j * STEP + at) * blocks + half * ROWS, ROWS)
                flat_ref[pl.ds(rows, ROWS), :] = outs[at]
            return tuple(after)

        lax.fori_loop(0, steps, back, start, unroll=4)
    for n in range(blocks):
        out_ref[n] = flat_ref[pl.ds(n, block_len, stride=blocks), :].T.astype(jnp.bfloat16)


def lag_sums(blocks, steps, x_ref, gt_ref, zero):
    lags = (zero,) * STEP
    for half in range(blocks // ROWS):

        def ahead(j, held):
            g = step_rows(gt_ref, j, blocks, half)
            x = step_rows(x_ref, j, blocks, half)
            return tuple(
                total + sum(g[i] * x[i - k] for i in range(k, STEP)) for k, total in enumerate(held)
            )

        lags = lax.fori_loop(0, steps, ahead, lags, unroll=8)
    return [jnp.sum(lag, axis=0, keepdims=True) for lag in lags]


def mode_sums(first, blocks, lags, x_ref, gt_ref, subs, lam_ref, h_ref, t_ref, parts_refs):
    modes = lam_ref.shape[0]
    block_len = gt_ref.shape[0] // blocks
    steps = block_len // STEP
    sub_ref, sub_t_ref = subs
    lam = lam_ref[first : first + GROUP, :]
    rate = log_rates(lam)
    empty = cleared(parts_refs[0], GROUP)
    wide = wide_rows(lam, 0, GROUP)
    jump = wide_rows(jnp.exp(STEP * rate), 0, GROUP)
    jump_slope = wide_rows(STEP * jnp.exp((STEP - 1) * rate), 0, GROUP)
    for half in range(blocks // ROWS):

        def ahead(j, held):
            x = step_rows(x_ref, j, blocks, half)[::-1]
            scaled = [k * x[k] for k in range(1, STEP)]
            state, slope, res_sum, pole_sum = [list(part) for part in held]
            for k in range(GROUP):
                rows = slot(j, blocks, half, modes, first + k)
                after = wide[k] * sub_ref[rows, :]
                res_sum[k] = res_sum[k] + state[k] * after
                pole_sum[k] = pole_sum[k] + (slope[k] * after + state[k] * sub_t_ref[rows, :])
                grown = jump[k] * slope[k] + jump_slope[k] * state[k]
                slope[k] = grown + horner(wide[k], scaled)
                state[k] = jump[k] * state[k] + horner(wide[k], x)
            return (tuple(state), tuple(slope), tuple(res_sum), tuple(pole_sum))

        results = lax.fori_loop(0, steps, ahead, (empty,) * 4, unroll=8)
        for ref, result in zip(parts_refs, results):
            put(ref, blocks, half, 0, result)
    block_step = jnp.exp(block_len * rate)
    block_slope = block_len * jnp.exp((block_len - 1) * rate)
    own = lambda ref, n: ref[pl.ds(n, GROUP, stride=blocks), :]
    of_all = lambda ref, n: ref[pl.ds(first * blocks + n, GROUP, stride=blocks), :]
    s_ref, d_ref, r_ref, q_ref = parts_refs
    state, slope, total, weighted = [jnp.zeros(lam.shape, F32)] * 4
    res_sum = horner(lam, lags)
    pole_sum = horner(lam, [k * lags[k] for k in range(1, STEP)])
    for n in range(blocks):
        after = lam * of_all(h_ref, n)
        res_sum = res_sum + (own(r_ref, n) + state * after)
        pole_sum = pole_sum + (own(q_ref, n) + slope * after + state * of_all(t_ref, n))
        slope = block_step * slope + block_slope * state + own(d_ref, n)
        state = block_step * state + own(s_ref, n)
    for n in range(blocks - 1, -1, -1):
        weighted = block_step * (weighted + block_len * total) + of_all(t_ref, n)
        total = block_step * total + of_all(h_ref, n)
    return state, slope, res_sum, pole_sum, weighted


def sums_kernel(blocks, shifts, *refs):
    pieces, refs = refs[: len(shifts) + 1], refs[len(shifts) + 1 :]
    gt_ref, sub_ref, sub_t_ref, lam_ref, h_ref, t_ref, pay_ref, moved_ref, xt_ref, *parts = refs
    modes = lam_ref.shape[0]
    chips = blocks // 2
    place = lax.axis_index("chan")
    chip, core = lax.div(place, 2), lax.rem(place, 2)
    for s, ref in zip((0, *shifts), pieces):
        source = 2 * lax.rem(chip + chips - s, chips)
        moved_ref[source + core] = ref[0]
        moved_ref[source + 1 - core] = ref[1]
    flip_blocks(moved_ref, xt_ref)
    steps = gt_ref.shape[0] // blocks // STEP
    lags = lag_sums(blocks, steps, xt_ref, gt_ref, cleared(parts[0], 1)[0])
    subs = (sub_ref, sub_t_ref)
    for first in range(0, modes, GROUP):
        items = mode_sums(first, blocks, lags, xt_ref, gt_ref, subs, lam_ref, h_ref, t_ref, parts)
        for k, item in enumerate(items):
            pay_ref[k * modes + first : k * modes + first + GROUP, :] = item


def ordered(refs, place, slots_ref):
    count = len(refs)
    for s, ref in enumerate(refs):
        slots_ref[lax.rem(place + count - s, count)] = ref[...]
    return [slots_ref[i] for i in range(count)]


def joined(lam, length, parts, heads):
    modes = lam.shape[0]
    rate = log_rates(lam)
    step = jnp.exp(length * rate)
    slope_step = length * jnp.exp((length - 1) * rate)
    state, slope, res_sum, pole_sum = [jnp.zeros(lam.shape, F32)] * 4
    tables = [[part[k * modes : (k + 1) * modes, :] for k in range(5)] for part in parts]
    for (ends, slopes, res_part, pole_part, weighted), head in zip(tables, heads):
        after = lam * head
        res_sum = res_sum + (res_part + state * after)
        pole_sum = pole_sum + (pole_part + slope * after + state * weighted)
        slope = step * slope + slope_step * state + slopes
        state = step * state + ends
    total = jnp.zeros(lam.shape, F32)
    weighted = total
    for table, head in zip(tables[::-1], heads[::-1]):
        weighted = step * (weighted + length * total) + table[4]
        total = step * total + head
    return state, slope, res_sum, pole_sum, weighted


def join_kernel(span_len, *refs):
    *parts, heads_ref, lam_ref, pay_ref, slots_ref = refs
    modes = lam_ref.shape[0]
    count = len(parts)
    place = lax.axis_index("len")
    parts = ordered(parts, lax.rem(place, count), slots_ref)
    heads = [heads_ref[place - lax.rem(place, count) + i] for i in range(count)]
    for k, item in enumerate(joined(lam_ref[...], span_len, parts, heads)):
        pay_ref[k * modes : (k + 1) * modes, :] = item


def finish_kernel(inner, span_len, *refs):
    *parts, heads_ref, lam_ref, res_ref, res_out, pole_out, slots_ref = refs
    count = len(parts)
    lam = lam_ref[...]
    step = jnp.exp(span_len * log_rates(lam))
    parts = ordered(parts, lax.div(lax.axis_index("len"), inner), slots_ref)
    heads = [
        folded(step, [heads_ref[g * inner + i] for i in range(inner)]) for g in range(count)
    ]
    _, _, res_sum, pole_sum, _ = joined(lam, inner * span_len, parts, heads)
    width = (1.0 - lam) * (1.0 + lam)
    scale = 1.0 / math.sqrt(count * inner * span_len)
    res_out[...] = res_sum * jnp.sqrt(width) * scale
    pole_out[...] = res_ref[...] * pole_sum * width * scale


def call(kernel, out_shape, in_count, scratch, name, flops, mebibytes=32):
    single = not isinstance(out_shape, (tuple, list))
    return pl.pallas_call(
        kernel,
        out_shape=out_shape,
        in_specs=[VMEM] * in_count,
        out_specs=VMEM if single else [VMEM] * len(out_shape),
        scratch_shapes=scratch,
        compiler_params=pltpu.CompilerParams(vmem_limit_bytes=mebibytes * 2**20),
        cost_estimate=pl.CostEstimate(flops=flops, bytes_accessed=2**20, transcendentals=0),
        name=name,
    )


def swap(part, axis):
    return lax.all_to_all(part, axis, split_axis=0, concat_axis=0, tiled=True)


def rotated(part, count, stride, spans):
    size = count * stride
    hop = lambda i, s: (i // size) * size + (i % size + s * stride) % size
    return [
        lax.ppermute(part, "len", [(i, hop(i, s)) for i in range(spans)]) for s in range(1, count)
    ]


def moved_pieces(part, blocks, shifts):
    chips = blocks // 2
    place = lax.axis_index("chan")
    chip, core = place // 2, place % 2
    got = lax.ppermute(part, "chan", [(i, i ^ 1) for i in range(blocks)])
    halves = [half.reshape(chips, 2, *half.shape[1:]) for half in (part, got)]
    block = lambda half, s: lax.dynamic_slice(
        half, ((chip + s) % chips, core, 0, 0), (1, 1, *half.shape[2:])
    )[0]
    at = lambda s: jnp.concatenate([block(half, s) for half in halves])
    ring = lambda s: [(i, (i + 2 * s) % blocks) for i in range(blocks)]
    return [at(0)] + [lax.ppermute(at(s), "chan", ring(s)) for s in shifts]


def body(inputs, grad_output, pole_values, residue_values):
    spans = lax.axis_size("len")
    blocks = lax.axis_size("chan")
    inner = math.isqrt(spans)
    outer = spans // inner
    chans, modes = pole_values.shape
    block_len = inputs.shape[1]
    flat = blocks * block_len
    held = modes * blocks
    work = chans * flat * modes
    shape = lambda *dims: jax.ShapeDtypeStruct(dims, F32)
    scratch = lambda *dims: pltpu.VMEM(dims, F32)
    cut = lambda part: part.reshape(blocks, chans, block_len)
    table = shape(modes, chans)
    poles = pole_values.T
    residues = residue_values.T
    moved_grads = swap(cut(grad_output), "chan")
    shifts = sorted(range(1, blocks // 2), key=lambda s: -min(s, blocks // 2 - s))
    pieces = moved_pieces(cut(inputs), blocks, shifts)
    flat_grads, ends, head = call(
        functools.partial(ends_kernel, blocks, spans),
        (
            jax.ShapeDtypeStruct((flat, chans), jnp.bfloat16),
            shape(held, chans),
            shape(spans, modes, chans),
        ),
        2,
        [scratch(flat, chans)],
        "block_ends",
        2 * work,
    )(moved_grads, poles)
    heads = swap(head, "len")
    subs = shape(held * block_len // STEP, chans)
    sub_heads, sub_weighted, weighted = call(
        functools.partial(weighted_kernel, blocks),
        (subs, subs, shape(held, chans)),
        2,
        [],
        "weighted",
        4 * work,
    )(flat_grads, poles)
    pay = call(
        functools.partial(sums_kernel, blocks, shifts),
        shape(5 * modes, chans),
        len(pieces) + 6,
        [pltpu.VMEM((blocks, chans, block_len), jnp.bfloat16), scratch(flat, chans)]
        + [scratch(GROUP * blocks, chans)] * 4,
        "mode_sums",
        8 * work,
    )(*pieces, flat_grads, sub_heads, sub_weighted, poles, ends, weighted)
    rounded = call(
        functools.partial(input_grad_kernel, blocks, spans),
        jax.ShapeDtypeStruct((blocks, chans, block_len), jnp.bfloat16),
        7,
        [scratch(held, chans), scratch(flat, chans)],
        "input_grad",
        4 * work,
    )(heads, flat_grads, sub_heads, poles, residues, ends, pay)
    input_grad = swap(rounded, "chan").reshape(blocks * chans, block_len)
    group_pay = call(
        functools.partial(join_kernel, flat),
        shape(5 * modes, chans),
        inner + 2,
        [scratch(inner, 5 * modes, chans)],
        "join",
        work // 100,
    )(pay, *rotated(pay, inner, 1, spans), heads, poles)
    residue_grad, pole_grad = call(
        functools.partial(finish_kernel, inner, flat),
        (table, table),
        outer + 3,
        [scratch(outer, 5 * modes, chans)],
        "finish",
        work // 100,
    )(group_pay, *rotated(group_pay, outer, inner, spans), heads, poles, residues)
    return (input_grad, residue_grad.T, pole_grad.T)


def solution(mesh):
    in_specs = (
        P(None, ("len", "chan")),
        P(None, ("len", "chan")),
        P("chan", None),
        P("chan", None),
    )
    out_specs = (P(None, ("len", "chan")), P("chan", None), P("chan", None))
    return jax.shard_map(body, mesh=mesh, in_specs=in_specs, out_specs=out_specs, check_vma=False)
```

```python
import functools
import math

import jax
import jax.numpy as jnp
from jax import lax
from jax.experimental import pallas as pl
from jax.experimental.pallas import tpu as pltpu
from jax.sharding import PartitionSpec as P

ROWS = 8
GROUP = 8
STEP = 8
F32 = jnp.float32
VMEM = pl.BlockSpec(memory_space=pltpu.VMEM)


def flip_blocks(src_ref, dst_ref):
    blocks, _, block_len = src_ref.shape
    for n in range(blocks):
        dst_ref[pl.ds(n, block_len, stride=blocks), :] = src_ref[n].astype(F32).T


def log_rates(poles):
    return jnp.log1p(-(1.0 - poles))


def cleared(ref, count):
    ref[:ROWS, :] = jnp.zeros((ROWS, ref.shape[1]), F32)
    return (ref[:ROWS, :],) * count


def block_rows(ref, n, blocks, modes):
    return ref[pl.ds(n, modes, stride=blocks), :]


def horner(rate, terms):
    total = terms[-1]
    for term in terms[-2::-1]:
        total = rate * total + term
    return total


def step_rows(ref, j, blocks, half):
    if ref.dtype == F32:
        at = lambda i: pl.multiple_of((j * STEP + i) * blocks + half * ROWS, ROWS)
        return [ref[pl.ds(at(i), ROWS), :] for i in range(STEP)]
    at = lambda i: pl.multiple_of((j * STEP + i) * blocks, blocks)
    rows = slice(half * ROWS, (half + 1) * ROWS)
    return [ref[pl.ds(at(i), blocks), :].astype(F32)[rows, :] for i in range(STEP)]


def slot(j, blocks, half, modes, p):
    at = ((j * (blocks // ROWS) + half) * modes + p) * ROWS
    return pl.ds(pl.multiple_of(at, ROWS), ROWS)


def wide_rows(table, first, count):
    return [jnp.broadcast_to(table[p : p + 1, :], (ROWS, table.shape[1])) for p in range(first, first + count)]


def put(ref, blocks, half, first, rows):
    for k, row in enumerate(rows):
        at = (first + k) * blocks + half * ROWS
        ref[at : at + ROWS, :] = row


def ends_kernel(blocks, spans, moved_ref, lam_ref, gt_ref, h_ref, head_ref, wide_ref):
    modes = lam_ref.shape[0]
    block_len = moved_ref.shape[2]
    steps = block_len // STEP
    flip_blocks(moved_ref, wide_ref)
    gt_ref[...] = wide_ref[...].astype(jnp.bfloat16)
    lam = lam_ref[...]
    rate = log_rates(lam)
    wide = wide_rows(lam, 0, modes)
    jump = wide_rows(jnp.exp(STEP * rate), 0, modes)
    empty = cleared(h_ref, modes)
    for half in range(blocks // ROWS):

        def back(i, held):
            j = steps - 1 - i
            g = step_rows(wide_ref, j, blocks, half)
            sums = [horner(l, g) for l in wide]
            return tuple(l * a + h for l, a, h in zip(jump, held, sums))

        put(h_ref, blocks, half, 0, lax.fori_loop(0, steps, back, empty, unroll=8))
    step = jnp.exp(block_len * rate)
    head = folded(step, [block_rows(h_ref, n, blocks, modes) for n in range(blocks)])
    for span in range(spans):
        head_ref[span] = head


def folded(step, heads):
    total = heads[-1]
    for head in heads[-2::-1]:
        total = step * total + head
    return total


def weighted_kernel(blocks, gt_ref, lam_ref, sub_ref, sub_t_ref, t_ref):
    modes = lam_ref.shape[0]
    steps = gt_ref.shape[0] // blocks // STEP
    lam = lam_ref[...]
    jumps = jnp.exp(STEP * log_rates(lam))
    empty = cleared(t_ref, modes)
    for first in range(0, modes, modes):
        wide = wide_rows(lam, first, modes)
        jump = wide_rows(jumps, first, modes)
        for half in range(blocks // ROWS):

            def back(i, held):
                j = steps - 1 - i
                g = step_rows(gt_ref, j, blocks, half)
                scaled = [(k + 1.0) * row for k, row in enumerate(g)]
                adjoint, weighted = held
                after, total = [], []
                for k in range(modes):
                    rows = slot(j, blocks, half, modes, first + k)
                    head = horner(wide[k], g)
                    part = horner(wide[k], scaled)
                    sub_ref[rows, :] = head
                    sub_t_ref[rows, :] = part
                    total.append(jump[k] * (weighted[k] + STEP * adjoint[k]) + part)
                    after.append(jump[k] * adjoint[k] + head)
                return (tuple(after), tuple(total))

            weighted = lax.fori_loop(0, steps, back, (empty,) * 2, unroll=2)[1]
            put(t_ref, blocks, half, first, weighted)


def folded_after(step, heads, place):
    total = jnp.zeros(step.shape, F32)
    for i in range(len(heads) - 1, 0, -1):
        total = jnp.where(i > place, step * total + heads[i], total)
    return total


def input_grad_kernel(
    blocks, spans, heads_ref, gt_ref, sub_ref, lam_ref, res_ref, h_ref, _, out_ref, next_ref, flat_ref
):
    modes = lam_ref.shape[0]
    block_len = gt_ref.shape[0] // blocks
    steps = block_len // STEP
    lam = lam_ref[...]
    res = res_ref[...]
    rate = log_rates(lam)
    block_step = jnp.exp(block_len * rate)
    span_step = jnp.exp((blocks * block_len) * rate)
    total = folded_after(span_step, [heads_ref[i] for i in range(spans)], lax.axis_index("len"))
    for n in range(blocks - 1, -1, -1):
        next_ref[pl.ds(n, modes, stride=blocks), :] = total
        total = block_step * total + block_rows(h_ref, n, blocks, modes)
    taps, power = [], res
    for _ in range(STEP):
        taps.append(jnp.broadcast_to(jnp.sum(power, axis=0, keepdims=True), (ROWS, lam.shape[1])))
        power = power * lam
    wide = wide_rows(lam, 0, modes)
    jump = wide_rows(jnp.exp(STEP * rate), 0, modes)
    gain = wide_rows(res, 0, modes)
    for half in range(blocks // ROWS):
        start = tuple(
            next_ref[p * blocks + half * ROWS : p * blocks + half * ROWS + ROWS, :]
            for p in range(modes)
        )

        def back(i, held):
            j = steps - 1 - i
            g = step_rows(gt_ref, j, blocks, half)
            outs = [sum(taps[k] * g[at + k] for k in range(STEP - at)) for at in range(STEP)]
            after = []
            for p in range(modes):
                term = gain[p] * held[p]
                for at in range(STEP - 1, -1, -1):
                    term = wide[p] * term
                    outs[at] = outs[at] + term
                after.append(jump[p] * held[p] + sub_ref[slot(j, blocks, half, modes, p), :])
            for at in range(STEP):
                rows = pl.multiple_of((j * STEP + at) * blocks + half * ROWS, ROWS)
                flat_ref[pl.ds(rows, ROWS), :] = outs[at]
            return tuple(after)

        lax.fori_loop(0, steps, back, start, unroll=4)
    for n in range(blocks):
        out_ref[n] = flat_ref[pl.ds(n, block_len, stride=blocks), :].T.astype(jnp.bfloat16)


def lag_sums(blocks, steps, x_ref, gt_ref, zero):
    lags = (zero,) * STEP
    for half in range(blocks // ROWS):

        def ahead(j, held):
            g = step_rows(gt_ref, j, blocks, half)
            x = step_rows(x_ref, j, blocks, half)
            return tuple(
                total + sum(g[i] * x[i - k] for i in range(k, STEP)) for k, total in enumerate(held)
            )

        lags = lax.fori_loop(0, steps, ahead, lags, unroll=8)
    return [jnp.sum(lag, axis=0, keepdims=True) for lag in lags]


def mode_sums(first, blocks, lags, x_ref, gt_ref, subs, lam_ref, h_ref, t_ref, parts_refs):
    modes = lam_ref.shape[0]
    block_len = gt_ref.shape[0] // blocks
    steps = block_len // STEP
    sub_ref, sub_t_ref = subs
    lam = lam_ref[first : first + GROUP, :]
    rate = log_rates(lam)
    empty = cleared(parts_refs[0], GROUP)
    wide = wide_rows(lam, 0, GROUP)
    jump = wide_rows(jnp.exp(STEP * rate), 0, GROUP)
    jump_slope = wide_rows(STEP * jnp.exp((STEP - 1) * rate), 0, GROUP)
    for half in range(blocks // ROWS):

        def ahead(j, held):
            x = step_rows(x_ref, j, blocks, half)[::-1]
            scaled = [k * x[k] for k in range(1, STEP)]
            state, slope, res_sum, pole_sum = [list(part) for part in held]
            for k in range(GROUP):
                rows = slot(j, blocks, half, modes, first + k)
                after = wide[k] * sub_ref[rows, :]
                res_sum[k] = res_sum[k] + state[k] * after
                pole_sum[k] = pole_sum[k] + (slope[k] * after + state[k] * sub_t_ref[rows, :])
                grown = jump[k] * slope[k] + jump_slope[k] * state[k]
                slope[k] = grown + horner(wide[k], scaled)
                state[k] = jump[k] * state[k] + horner(wide[k], x)
            return (tuple(state), tuple(slope), tuple(res_sum), tuple(pole_sum))

        results = lax.fori_loop(0, steps, ahead, (empty,) * 4, unroll=8)
        for ref, result in zip(parts_refs, results):
            put(ref, blocks, half, 0, result)
    block_step = jnp.exp(block_len * rate)
    block_slope = block_len * jnp.exp((block_len - 1) * rate)
    own = lambda ref, n: ref[pl.ds(n, GROUP, stride=blocks), :]
    of_all = lambda ref, n: ref[pl.ds(first * blocks + n, GROUP, stride=blocks), :]
    s_ref, d_ref, r_ref, q_ref = parts_refs
    state, slope, total, weighted = [jnp.zeros(lam.shape, F32)] * 4
    res_sum = horner(lam, lags)
    pole_sum = horner(lam, [k * lags[k] for k in range(1, STEP)])
    for n in range(blocks):
        after = lam * of_all(h_ref, n)
        res_sum = res_sum + (own(r_ref, n) + state * after)
        pole_sum = pole_sum + (own(q_ref, n) + slope * after + state * of_all(t_ref, n))
        slope = block_step * slope + block_slope * state + own(d_ref, n)
        state = block_step * state + own(s_ref, n)
    for n in range(blocks - 1, -1, -1):
        weighted = block_step * (weighted + block_len * total) + of_all(t_ref, n)
        total = block_step * total + of_all(h_ref, n)
    return state, slope, res_sum, pole_sum, weighted


def sums_kernel(blocks, shifts, *refs):
    pieces, refs = refs[: len(shifts) + 1], refs[len(shifts) + 1 :]
    gt_ref, sub_ref, sub_t_ref, lam_ref, h_ref, t_ref, pay_ref, moved_ref, xt_ref, *parts = refs
    modes = lam_ref.shape[0]
    chips = blocks // 2
    place = lax.axis_index("chan")
    chip, core = lax.div(place, 2), lax.rem(place, 2)
    for s, ref in zip((0, *shifts), pieces):
        source = 2 * lax.rem(chip + chips - s, chips)
        moved_ref[source + core] = ref[0]
        moved_ref[source + 1 - core] = ref[1]
    flip_blocks(moved_ref, xt_ref)
    steps = gt_ref.shape[0] // blocks // STEP
    lags = lag_sums(blocks, steps, xt_ref, gt_ref, cleared(parts[0], 1)[0])
    subs = (sub_ref, sub_t_ref)
    for first in range(0, modes, GROUP):
        items = mode_sums(first, blocks, lags, xt_ref, gt_ref, subs, lam_ref, h_ref, t_ref, parts)
        for k, item in enumerate(items):
            pay_ref[k * modes + first : k * modes + first + GROUP, :] = item


def ordered(refs, place, slots_ref):
    count = len(refs)
    for s, ref in enumerate(refs):
        slots_ref[lax.rem(place + count - s, count)] = ref[...]
    return [slots_ref[i] for i in range(count)]


def joined(lam, length, parts, heads):
    modes = lam.shape[0]
    rate = log_rates(lam)
    step = jnp.exp(length * rate)
    slope_step = length * jnp.exp((length - 1) * rate)
    state, slope, res_sum, pole_sum = [jnp.zeros(lam.shape, F32)] * 4
    tables = [[part[k * modes : (k + 1) * modes, :] for k in range(5)] for part in parts]
    for (ends, slopes, res_part, pole_part, weighted), head in zip(tables, heads):
        after = lam * head
        res_sum = res_sum + (res_part + state * after)
        pole_sum = pole_sum + (pole_part + slope * after + state * weighted)
        slope = step * slope + slope_step * state + slopes
        state = step * state + ends
    total = jnp.zeros(lam.shape, F32)
    weighted = total
    for table, head in zip(tables[::-1], heads[::-1]):
        weighted = step * (weighted + length * total) + table[4]
        total = step * total + head
    return state, slope, res_sum, pole_sum, weighted


def join_kernel(span_len, *refs):
    *parts, heads_ref, lam_ref, pay_ref, slots_ref = refs
    modes = lam_ref.shape[0]
    count = len(parts)
    place = lax.axis_index("len")
    parts = ordered(parts, lax.rem(place, count), slots_ref)
    heads = [heads_ref[place - lax.rem(place, count) + i] for i in range(count)]
    for k, item in enumerate(joined(lam_ref[...], span_len, parts, heads)):
        pay_ref[k * modes : (k + 1) * modes, :] = item


def finish_kernel(inner, span_len, *refs):
    *parts, heads_ref, lam_ref, res_ref, res_out, pole_out, slots_ref = refs
    count = len(parts)
    lam = lam_ref[...]
    step = jnp.exp(span_len * log_rates(lam))
    parts = ordered(parts, lax.div(lax.axis_index("len"), inner), slots_ref)
    heads = [
        folded(step, [heads_ref[g * inner + i] for i in range(inner)]) for g in range(count)
    ]
    _, _, res_sum, pole_sum, _ = joined(lam, inner * span_len, parts, heads)
    width = (1.0 - lam) * (1.0 + lam)
    scale = 1.0 / math.sqrt(count * inner * span_len)
    res_out[...] = res_sum * jnp.sqrt(width) * scale
    pole_out[...] = res_ref[...] * pole_sum * width * scale


def call(kernel, out_shape, in_count, scratch, name, flops, mebibytes=32):
    single = not isinstance(out_shape, (tuple, list))
    return pl.pallas_call(
        kernel,
        out_shape=out_shape,
        in_specs=[VMEM] * in_count,
        out_specs=VMEM if single else [VMEM] * len(out_shape),
        scratch_shapes=scratch,
        compiler_params=pltpu.CompilerParams(vmem_limit_bytes=mebibytes * 2**20),
        cost_estimate=pl.CostEstimate(flops=flops, bytes_accessed=2**20, transcendentals=0),
        name=name,
    )


def swap(part, axis):
    return lax.all_to_all(part, axis, split_axis=0, concat_axis=0, tiled=True)


def rotated(part, count, stride, spans):
    size = count * stride
    hop = lambda i, s: (i // size) * size + (i % size + s * stride) % size
    return [
        lax.ppermute(part, "len", [(i, hop(i, s)) for i in range(spans)]) for s in range(1, count)
    ]


def moved_pieces(part, blocks, shifts):
    chips = blocks // 2
    place = lax.axis_index("chan")
    chip, core = place // 2, place % 2
    got = lax.ppermute(part, "chan", [(i, i ^ 1) for i in range(blocks)])
    halves = [half.reshape(chips, 2, *half.shape[1:]) for half in (part, got)]
    block = lambda half, s: lax.dynamic_slice(
        half, ((chip + s) % chips, core, 0, 0), (1, 1, *half.shape[2:])
    )[0]
    at = lambda s: jnp.concatenate([block(half, s) for half in halves])
    ring = lambda s: [(i, (i + 2 * s) % blocks) for i in range(blocks)]
    return [at(0)] + [lax.ppermute(at(s), "chan", ring(s)) for s in shifts]


def body(inputs, grad_output, pole_values, residue_values):
    spans = lax.axis_size("len")
    blocks = lax.axis_size("chan")
    inner = math.isqrt(spans)
    outer = spans // inner
    chans, modes = pole_values.shape
    block_len = inputs.shape[1]
    flat = blocks * block_len
    held = modes * blocks
    work = chans * flat * modes
    shape = lambda *dims: jax.ShapeDtypeStruct(dims, F32)
    scratch = lambda *dims: pltpu.VMEM(dims, F32)
    cut = lambda part: part.reshape(blocks, chans, block_len)
    table = shape(modes, chans)
    poles = pole_values.T
    residues = residue_values.T
    moved_grads = swap(cut(grad_output), "chan")
    shifts = sorted(range(1, blocks // 2), key=lambda s: -min(s, blocks // 2 - s))
    pieces = moved_pieces(cut(inputs), blocks, shifts)
    flat_grads, ends, head = call(
        functools.partial(ends_kernel, blocks, spans),
        (
            jax.ShapeDtypeStruct((flat, chans), jnp.bfloat16),
            shape(held, chans),
            shape(spans, modes, chans),
        ),
        2,
        [scratch(flat, chans)],
        "block_ends",
        2 * work,
    )(moved_grads, poles)
    heads = swap(head, "len")
    subs = shape(held * block_len // STEP, chans)
    sub_heads, sub_weighted, weighted = call(
        functools.partial(weighted_kernel, blocks),
        (subs, subs, shape(held, chans)),
        2,
        [],
        "weighted",
        4 * work,
    )(flat_grads, poles)
    pay = call(
        functools.partial(sums_kernel, blocks, shifts),
        shape(5 * modes, chans),
        len(pieces) + 6,
        [pltpu.VMEM((blocks, chans, block_len), jnp.bfloat16), scratch(flat, chans)]
        + [scratch(GROUP * blocks, chans)] * 4,
        "mode_sums",
        8 * work,
    )(*pieces, flat_grads, sub_heads, sub_weighted, poles, ends, weighted)
    rounded = call(
        functools.partial(input_grad_kernel, blocks, spans),
        jax.ShapeDtypeStruct((blocks, chans, block_len), jnp.bfloat16),
        7,
        [scratch(held, chans), scratch(flat, chans)],
        "input_grad",
        4 * work,
    )(heads, flat_grads, sub_heads, poles, residues, ends, pay)
    input_grad = swap(rounded, "chan").reshape(blocks * chans, block_len)
    group_pay = call(
        functools.partial(join_kernel, flat),
        shape(5 * modes, chans),
        inner + 2,
        [scratch(inner, 5 * modes, chans)],
        "join",
        work // 100,
    )(pay, *rotated(pay, inner, 1, spans), heads, poles)
    residue_grad, pole_grad = call(
        functools.partial(finish_kernel, inner, flat),
        (table, table),
        outer + 3,
        [scratch(outer, 5 * modes, chans)],
        "finish",
        work // 100,
    )(group_pay, *rotated(group_pay, outer, inner, spans), heads, poles, residues)
    return (input_grad, residue_grad.T, pole_grad.T)


def solution(mesh):
    in_specs = (
        P(None, ("len", "chan")),
        P(None, ("len", "chan")),
        P("chan", None),
        P("chan", None),
    )
    out_specs = (P(None, ("len", "chan")), P("chan", None), P("chan", None))
    return jax.shard_map(body, mesh=mesh, in_specs=in_specs, out_specs=out_specs, check_vma=False)
```

```python
import functools
import math

import jax
import jax.numpy as jnp
from jax import lax
from jax.experimental import pallas as pl
from jax.experimental.pallas import tpu as pltpu
from jax.sharding import PartitionSpec as P

ROWS = 8
GROUP = 8
STEP = 8
F32 = jnp.float32
VMEM = pl.BlockSpec(memory_space=pltpu.VMEM)


def flip_blocks(src_ref, dst_ref):
    blocks, _, block_len = src_ref.shape
    for n in range(blocks):
        dst_ref[pl.ds(n, block_len, stride=blocks), :] = src_ref[n].astype(F32).T


def log_rates(poles):
    return jnp.log1p(-(1.0 - poles))


def cleared(ref, count):
    ref[:ROWS, :] = jnp.zeros((ROWS, ref.shape[1]), F32)
    return (ref[:ROWS, :],) * count


def block_rows(ref, n, blocks, modes):
    return ref[pl.ds(n, modes, stride=blocks), :]


def horner(rate, terms):
    total = terms[-1]
    for term in terms[-2::-1]:
        total = rate * total + term
    return total


def step_rows(ref, j, blocks, half):
    if ref.dtype == F32:
        at = lambda i: pl.multiple_of((j * STEP + i) * blocks + half * ROWS, ROWS)
        return [ref[pl.ds(at(i), ROWS), :] for i in range(STEP)]
    at = lambda i: pl.multiple_of((j * STEP + i) * blocks, blocks)
    rows = slice(half * ROWS, (half + 1) * ROWS)
    return [ref[pl.ds(at(i), blocks), :].astype(F32)[rows, :] for i in range(STEP)]


def slot(j, blocks, half, modes, p):
    at = ((j * (blocks // ROWS) + half) * modes + p) * ROWS
    return pl.ds(pl.multiple_of(at, ROWS), ROWS)


def wide_rows(table, first, count):
    return [jnp.broadcast_to(table[p : p + 1, :], (ROWS, table.shape[1])) for p in range(first, first + count)]


def put(ref, blocks, half, first, rows):
    for k, row in enumerate(rows):
        at = (first + k) * blocks + half * ROWS
        ref[at : at + ROWS, :] = row


def ends_kernel(blocks, spans, moved_ref, lam_ref, gt_ref, h_ref, head_ref, wide_ref):
    modes = lam_ref.shape[0]
    block_len = moved_ref.shape[2]
    steps = block_len // STEP
    flip_blocks(moved_ref, wide_ref)
    gt_ref[...] = wide_ref[...].astype(jnp.bfloat16)
    lam = lam_ref[...]
    rate = log_rates(lam)
    wide = wide_rows(lam, 0, modes)
    jump = wide_rows(jnp.exp(STEP * rate), 0, modes)
    empty = cleared(h_ref, modes)
    for half in range(blocks // ROWS):

        def back(i, held):
            j = steps - 1 - i
            g = step_rows(wide_ref, j, blocks, half)
            sums = [horner(l, g) for l in wide]
            return tuple(l * a + h for l, a, h in zip(jump, held, sums))

        put(h_ref, blocks, half, 0, lax.fori_loop(0, steps, back, empty, unroll=16))
    step = jnp.exp(block_len * rate)
    head = folded(step, [block_rows(h_ref, n, blocks, modes) for n in range(blocks)])
    for span in range(spans):
        head_ref[span] = head


def folded(step, heads):
    total = heads[-1]
    for head in heads[-2::-1]:
        total = step * total + head
    return total


def weighted_kernel(blocks, gt_ref, lam_ref, sub_ref, sub_t_ref, t_ref):
    modes = lam_ref.shape[0]
    steps = gt_ref.shape[0] // blocks // STEP
    lam = lam_ref[...]
    jumps = jnp.exp(STEP * log_rates(lam))
    empty = cleared(t_ref, modes)
    for first in range(0, modes, modes):
        wide = wide_rows(lam, first, modes)
        jump = wide_rows(jumps, first, modes)
        for half in range(blocks // ROWS):

            def back(i, held):
                j = steps - 1 - i
                g = step_rows(gt_ref, j, blocks, half)
                scaled = [(k + 1.0) * row for k, row in enumerate(g)]
                adjoint, weighted = held
                after, total = [], []
                for k in range(modes):
                    rows = slot(j, blocks, half, modes, first + k)
                    head = horner(wide[k], g)
                    part = horner(wide[k], scaled)
                    sub_ref[rows, :] = head
                    sub_t_ref[rows, :] = part
                    total.append(jump[k] * (weighted[k] + STEP * adjoint[k]) + part)
                    after.append(jump[k] * adjoint[k] + head)
                return (tuple(after), tuple(total))

            weighted = lax.fori_loop(0, steps, back, (empty,) * 2, unroll=2)[1]
            put(t_ref, blocks, half, first, weighted)


def folded_after(step, heads, place):
    total = jnp.zeros(step.shape, F32)
    for i in range(len(heads) - 1, 0, -1):
        total = jnp.where(i > place, step * total + heads[i], total)
    return total


def input_grad_kernel(
    blocks, spans, heads_ref, gt_ref, sub_ref, lam_ref, res_ref, h_ref, _, out_ref, next_ref, flat_ref
):
    modes = lam_ref.shape[0]
    block_len = gt_ref.shape[0] // blocks
    steps = block_len // STEP
    lam = lam_ref[...]
    res = res_ref[...]
    rate = log_rates(lam)
    block_step = jnp.exp(block_len * rate)
    span_step = jnp.exp((blocks * block_len) * rate)
    total = folded_after(span_step, [heads_ref[i] for i in range(spans)], lax.axis_index("len"))
    for n in range(blocks - 1, -1, -1):
        next_ref[pl.ds(n, modes, stride=blocks), :] = total
        total = block_step * total + block_rows(h_ref, n, blocks, modes)
    taps, power = [], res
    for _ in range(STEP):
        taps.append(jnp.broadcast_to(jnp.sum(power, axis=0, keepdims=True), (ROWS, lam.shape[1])))
        power = power * lam
    wide = wide_rows(lam, 0, modes)
    jump = wide_rows(jnp.exp(STEP * rate), 0, modes)
    gain = wide_rows(res, 0, modes)
    for half in range(blocks // ROWS):
        start = tuple(
            next_ref[p * blocks + half * ROWS : p * blocks + half * ROWS + ROWS, :]
            for p in range(modes)
        )

        def back(i, held):
            j = steps - 1 - i
            g = step_rows(gt_ref, j, blocks, half)
            outs = [sum(taps[k] * g[at + k] for k in range(STEP - at)) for at in range(STEP)]
            after = []
            for p in range(modes):
                term = gain[p] * held[p]
                for at in range(STEP - 1, -1, -1):
                    term = wide[p] * term
                    outs[at] = outs[at] + term
                after.append(jump[p] * held[p] + sub_ref[slot(j, blocks, half, modes, p), :])
            for at in range(STEP):
                rows = pl.multiple_of((j * STEP + at) * blocks + half * ROWS, ROWS)
                flat_ref[pl.ds(rows, ROWS), :] = outs[at]
            return tuple(after)

        lax.fori_loop(0, steps, back, start, unroll=8)
    for n in range(blocks):
        out_ref[n] = flat_ref[pl.ds(n, block_len, stride=blocks), :].T.astype(jnp.bfloat16)


def lag_sums(blocks, steps, x_ref, gt_ref, zero):
    lags = (zero,) * STEP
    for half in range(blocks // ROWS):

        def ahead(j, held):
            g = step_rows(gt_ref, j, blocks, half)
            x = step_rows(x_ref, j, blocks, half)
            return tuple(
                total + sum(g[i] * x[i - k] for i in range(k, STEP)) for k, total in enumerate(held)
            )

        lags = lax.fori_loop(0, steps, ahead, lags, unroll=8)
    return [jnp.sum(lag, axis=0, keepdims=True) for lag in lags]


def mode_sums(first, blocks, lags, x_ref, gt_ref, subs, lam_ref, h_ref, t_ref, parts_refs):
    modes = lam_ref.shape[0]
    block_len = gt_ref.shape[0] // blocks
    steps = block_len // STEP
    sub_ref, sub_t_ref = subs
    lam = lam_ref[first : first + GROUP, :]
    rate = log_rates(lam)
    empty = cleared(parts_refs[0], GROUP)
    wide = wide_rows(lam, 0, GROUP)
    jump = wide_rows(jnp.exp(STEP * rate), 0, GROUP)
    jump_slope = wide_rows(STEP * jnp.exp((STEP - 1) * rate), 0, GROUP)
    for half in range(blocks // ROWS):

        def ahead(j, held):
            x = step_rows(x_ref, j, blocks, half)[::-1]
            scaled = [k * x[k] for k in range(1, STEP)]
            state, slope, res_sum, pole_sum = [list(part) for part in held]
            for k in range(GROUP):
                rows = slot(j, blocks, half, modes, first + k)
                after = wide[k] * sub_ref[rows, :]
                res_sum[k] = res_sum[k] + state[k] * after
                pole_sum[k] = pole_sum[k] + (slope[k] * after + state[k] * sub_t_ref[rows, :])
                grown = jump[k] * slope[k] + jump_slope[k] * state[k]
                slope[k] = grown + horner(wide[k], scaled)
                state[k] = jump[k] * state[k] + horner(wide[k], x)
            return (tuple(state), tuple(slope), tuple(res_sum), tuple(pole_sum))

        results = lax.fori_loop(0, steps, ahead, (empty,) * 4, unroll=16)
        for ref, result in zip(parts_refs, results):
            put(ref, blocks, half, 0, result)
    block_step = jnp.exp(block_len * rate)
    block_slope = block_len * jnp.exp((block_len - 1) * rate)
    own = lambda ref, n: ref[pl.ds(n, GROUP, stride=blocks), :]
    of_all = lambda ref, n: ref[pl.ds(first * blocks + n, GROUP, stride=blocks), :]
    s_ref, d_ref, r_ref, q_ref = parts_refs
    state, slope, total, weighted = [jnp.zeros(lam.shape, F32)] * 4
    res_sum = horner(lam, lags)
    pole_sum = horner(lam, [k * lags[k] for k in range(1, STEP)])
    for n in range(blocks):
        after = lam * of_all(h_ref, n)
        res_sum = res_sum + (own(r_ref, n) + state * after)
        pole_sum = pole_sum + (own(q_ref, n) + slope * after + state * of_all(t_ref, n))
        slope = block_step * slope + block_slope * state + own(d_ref, n)
        state = block_step * state + own(s_ref, n)
    for n in range(blocks - 1, -1, -1):
        weighted = block_step * (weighted + block_len * total) + of_all(t_ref, n)
        total = block_step * total + of_all(h_ref, n)
    return state, slope, res_sum, pole_sum, weighted


def sums_kernel(blocks, shifts, *refs):
    pieces, refs = refs[: len(shifts) + 1], refs[len(shifts) + 1 :]
    gt_ref, sub_ref, sub_t_ref, lam_ref, h_ref, t_ref, pay_ref, moved_ref, xt_ref, *parts = refs
    modes = lam_ref.shape[0]
    chips = blocks // 2
    place = lax.axis_index("chan")
    chip, core = lax.div(place, 2), lax.rem(place, 2)
    for s, ref in zip((0, *shifts), pieces):
        source = 2 * lax.rem(chip + chips - s, chips)
        moved_ref[source + core] = ref[0]
        moved_ref[source + 1 - core] = ref[1]
    flip_blocks(moved_ref, xt_ref)
    steps = gt_ref.shape[0] // blocks // STEP
    lags = lag_sums(blocks, steps, xt_ref, gt_ref, cleared(parts[0], 1)[0])
    subs = (sub_ref, sub_t_ref)
    for first in range(0, modes, GROUP):
        items = mode_sums(first, blocks, lags, xt_ref, gt_ref, subs, lam_ref, h_ref, t_ref, parts)
        for k, item in enumerate(items):
            pay_ref[k * modes + first : k * modes + first + GROUP, :] = item


def ordered(refs, place, slots_ref):
    count = len(refs)
    for s, ref in enumerate(refs):
        slots_ref[lax.rem(place + count - s, count)] = ref[...]
    return [slots_ref[i] for i in range(count)]


def joined(lam, length, parts, heads):
    modes = lam.shape[0]
    rate = log_rates(lam)
    step = jnp.exp(length * rate)
    slope_step = length * jnp.exp((length - 1) * rate)
    state, slope, res_sum, pole_sum = [jnp.zeros(lam.shape, F32)] * 4
    tables = [[part[k * modes : (k + 1) * modes, :] for k in range(5)] for part in parts]
    for (ends, slopes, res_part, pole_part, weighted), head in zip(tables, heads):
        after = lam * head
        res_sum = res_sum + (res_part + state * after)
        pole_sum = pole_sum + (pole_part + slope * after + state * weighted)
        slope = step * slope + slope_step * state + slopes
        state = step * state + ends
    total = jnp.zeros(lam.shape, F32)
    weighted = total
    for table, head in zip(tables[::-1], heads[::-1]):
        weighted = step * (weighted + length * total) + table[4]
        total = step * total + head
    return state, slope, res_sum, pole_sum, weighted


def join_kernel(span_len, *refs):
    *parts, heads_ref, lam_ref, pay_ref, slots_ref = refs
    modes = lam_ref.shape[0]
    count = len(parts)
    place = lax.axis_index("len")
    parts = ordered(parts, lax.rem(place, count), slots_ref)
    heads = [heads_ref[place - lax.rem(place, count) + i] for i in range(count)]
    for k, item in enumerate(joined(lam_ref[...], span_len, parts, heads)):
        pay_ref[k * modes : (k + 1) * modes, :] = item


def finish_kernel(inner, span_len, *refs):
    *parts, heads_ref, lam_ref, res_ref, res_out, pole_out, slots_ref = refs
    count = len(parts)
    lam = lam_ref[...]
    step = jnp.exp(span_len * log_rates(lam))
    parts = ordered(parts, lax.div(lax.axis_index("len"), inner), slots_ref)
    heads = [
        folded(step, [heads_ref[g * inner + i] for i in range(inner)]) for g in range(count)
    ]
    _, _, res_sum, pole_sum, _ = joined(lam, inner * span_len, parts, heads)
    width = (1.0 - lam) * (1.0 + lam)
    scale = 1.0 / math.sqrt(count * inner * span_len)
    res_out[...] = res_sum * jnp.sqrt(width) * scale
    pole_out[...] = res_ref[...] * pole_sum * width * scale


def call(kernel, out_shape, in_count, scratch, name, flops, mebibytes=32):
    single = not isinstance(out_shape, (tuple, list))
    return pl.pallas_call(
        kernel,
        out_shape=out_shape,
        in_specs=[VMEM] * in_count,
        out_specs=VMEM if single else [VMEM] * len(out_shape),
        scratch_shapes=scratch,
        compiler_params=pltpu.CompilerParams(vmem_limit_bytes=mebibytes * 2**20),
        cost_estimate=pl.CostEstimate(flops=flops, bytes_accessed=2**20, transcendentals=0),
        name=name,
    )


def swap(part, axis):
    return lax.all_to_all(part, axis, split_axis=0, concat_axis=0, tiled=True)


def rotated(part, count, stride, spans):
    size = count * stride
    hop = lambda i, s: (i // size) * size + (i % size + s * stride) % size
    return [
        lax.ppermute(part, "len", [(i, hop(i, s)) for i in range(spans)]) for s in range(1, count)
    ]


def moved_pieces(part, blocks, shifts):
    chips = blocks // 2
    place = lax.axis_index("chan")
    chip, core = place // 2, place % 2
    got = lax.ppermute(part, "chan", [(i, i ^ 1) for i in range(blocks)])
    halves = [half.reshape(chips, 2, *half.shape[1:]) for half in (part, got)]
    block = lambda half, s: lax.dynamic_slice(
        half, ((chip + s) % chips, core, 0, 0), (1, 1, *half.shape[2:])
    )[0]
    at = lambda s: jnp.concatenate([block(half, s) for half in halves])
    ring = lambda s: [(i, (i + 2 * s) % blocks) for i in range(blocks)]
    return [at(0)] + [lax.ppermute(at(s), "chan", ring(s)) for s in shifts]


def body(inputs, grad_output, pole_values, residue_values):
    spans = lax.axis_size("len")
    blocks = lax.axis_size("chan")
    inner = math.isqrt(spans)
    outer = spans // inner
    chans, modes = pole_values.shape
    block_len = inputs.shape[1]
    flat = blocks * block_len
    held = modes * blocks
    work = chans * flat * modes
    shape = lambda *dims: jax.ShapeDtypeStruct(dims, F32)
    scratch = lambda *dims: pltpu.VMEM(dims, F32)
    cut = lambda part: part.reshape(blocks, chans, block_len)
    table = shape(modes, chans)
    poles = pole_values.T
    residues = residue_values.T
    moved_grads = swap(cut(grad_output), "chan")
    shifts = sorted(range(1, blocks // 2), key=lambda s: -min(s, blocks // 2 - s))
    pieces = moved_pieces(cut(inputs), blocks, shifts)
    flat_grads, ends, head = call(
        functools.partial(ends_kernel, blocks, spans),
        (
            jax.ShapeDtypeStruct((flat, chans), jnp.bfloat16),
            shape(held, chans),
            shape(spans, modes, chans),
        ),
        2,
        [scratch(flat, chans)],
        "block_ends",
        2 * work,
    )(moved_grads, poles)
    heads = swap(head, "len")
    subs = shape(held * block_len // STEP, chans)
    sub_heads, sub_weighted, weighted = call(
        functools.partial(weighted_kernel, blocks),
        (subs, subs, shape(held, chans)),
        2,
        [],
        "weighted",
        4 * work,
    )(flat_grads, poles)
    pay = call(
        functools.partial(sums_kernel, blocks, shifts),
        shape(5 * modes, chans),
        len(pieces) + 6,
        [pltpu.VMEM((blocks, chans, block_len), jnp.bfloat16), scratch(flat, chans)]
        + [scratch(GROUP * blocks, chans)] * 4,
        "mode_sums",
        8 * work,
    )(*pieces, flat_grads, sub_heads, sub_weighted, poles, ends, weighted)
    rounded = call(
        functools.partial(input_grad_kernel, blocks, spans),
        jax.ShapeDtypeStruct((blocks, chans, block_len), jnp.bfloat16),
        7,
        [scratch(held, chans), scratch(flat, chans)],
        "input_grad",
        4 * work,
    )(heads, flat_grads, sub_heads, poles, residues, ends, pay)
    input_grad = swap(rounded, "chan").reshape(blocks * chans, block_len)
    group_pay = call(
        functools.partial(join_kernel, flat),
        shape(5 * modes, chans),
        inner + 2,
        [scratch(inner, 5 * modes, chans)],
        "join",
        work // 100,
    )(pay, *rotated(pay, inner, 1, spans), heads, poles)
    residue_grad, pole_grad = call(
        functools.partial(finish_kernel, inner, flat),
        (table, table),
        outer + 3,
        [scratch(outer, 5 * modes, chans)],
        "finish",
        work // 100,
    )(group_pay, *rotated(group_pay, outer, inner, spans), heads, poles, residues)
    return (input_grad, residue_grad.T, pole_grad.T)


def solution(mesh):
    in_specs = (
        P(None, ("len", "chan")),
        P(None, ("len", "chan")),
        P("chan", None),
        P("chan", None),
    )
    out_specs = (P(None, ("len", "chan")), P("chan", None), P("chan", None))
    return jax.shard_map(body, mesh=mesh, in_specs=in_specs, out_specs=out_specs, check_vma=False)
```
